32 devices in a mesh: team: 8 (over y, x, core), rep: 4 (over z).
Axes of the slice: x: 2, y: 2, z: 4, core: 2. Of those that a mesh axis runs over, the one named last changes fastest.
Arguments:
- points: bfloat16 [8192, 128], P('team'), may hold values from -3 to 3
Outputs:
- potential: float32 [8192], P('team')
- displacement: float32 [8192, 128], P('team')
The draws below stay inside these ranges and needn't reach their ends.
All inputs are finite; a program needn't handle non-finite values.
Results may differ from the reference program's by a relative error of at most 0.0097.
The reference program's roundings to bfloat16 on the way (of `rounded`) count: a program that leaves them out, or rounds other values in their place, can miss the bound.
Values may be sent and summed in bfloat16 or wider, within the bound.
No kernel may reach another device: no remote copies, remote signals or barrier semaphores. Data moves between devices by JAX's collectives and lax.ppermute only.
A program may use at most 64 MiB of HBM per device.

```python
import math
import jax
import jax.numpy as jnp
from jax import lax

D = 128
TEAM_PTS = 1024
NPTS = 8192
N_TEAM = 8


def draw_points(key, part):
    base_key = jax.random.fold_in(key, 11)
    scale_key = jax.random.fold_in(key, 23)
    center_key = jax.random.fold_in(key, 37)
    label_key = jax.random.fold_in(key, 41)
    clusters = 8
    labels = jax.random.randint(label_key, (NPTS,), 0, clusters)
    centers = jax.random.normal(center_key, (clusters, D), jnp.float32) * 0.3
    values = jax.random.normal(base_key, (NPTS, D), jnp.float32)
    scales = jnp.exp(jax.random.uniform(scale_key, (NPTS, 1), jnp.float32, -0.35, 0.35))
    noise = values * scales * (2.8 / math.sqrt(D))
    shared = jnp.take(centers, labels, axis=0)
    return jnp.clip(shared + noise, -3.0, 3.0).astype(jnp.bfloat16)


def setup_inputs(seed: int = 0) -> dict:
    keys = jax.random.split(jax.random.key(seed), 2)
    points = draw_points(jax.random.fold_in(keys[1], 71), 0)
    return dict(points=points)


def row_sums(points_wide, sq_norm, potentials, inv_eps, with_num):
    blocks = points_wide.reshape(N_TEAM, TEAM_PTS, D)
    sq_blocks = sq_norm.reshape(N_TEAM, TEAM_PTS)

    def one_block(inputs):
        row_points, row_sq = inputs
        products = jnp.dot(row_points, points_wide.T, precision=lax.Precision.HIGHEST, preferred_element_type=jnp.float32)
        cost_tile = 0.5 * row_sq[:, None] + 0.5 * sq_norm[None, :] - products
        kernel = jnp.exp((potentials[None, :] - cost_tile) * inv_eps)
        row_total = jnp.sum(kernel, axis=1)
        if with_num:
            rounded = lax.optimization_barrier(kernel.astype(jnp.bfloat16)).astype(jnp.float32)
            numerator = jnp.dot(rounded, points_wide, precision=lax.Precision.HIGHEST, preferred_element_type=jnp.float32)
            return row_total, numerator
        return row_total, row_total

    totals, numerators = lax.map(one_block, (blocks, sq_blocks))
    if with_num:
        return totals.reshape(NPTS), numerators.reshape(NPTS, D)
    return totals.reshape(NPTS), totals.reshape(NPTS)


def reference(points):
    points_wide = points.astype(jnp.float32)
    sq_norm = jnp.sum(points_wide * points_wide, axis=1)
    log_count = jnp.log(jnp.float32(NPTS))
    zero_pot = jnp.zeros((NPTS,), jnp.float32)
    first_sum, unused_rows = row_sums(points_wide, sq_norm, zero_pot, 0.25, False)
    pot_one = 0.5 * (zero_pot - 4.0 * (jnp.log(first_sum) - log_count))
    second, numerator = row_sums(points_wide, sq_norm, pot_one, 0.5, True)
    potential = 0.5 * (pot_one - 2.0 * (jnp.log(second) - log_count))
    displacement = points_wide - numerator / second[:, None]
    return potential, displacement
```

```python
import functools
import jax
import jax.numpy as jnp
from jax import lax
from jax.experimental import pallas as pl
from jax.experimental.pallas import tpu as pltpu
from jax.sharding import PartitionSpec as P

F32 = jnp.float32
BF16 = jnp.bfloat16
NT = (((1,), (1,)), ((), ()))
IN_VMEM = pl.BlockSpec(memory_space=pltpu.VMEM)
IN_HBM = pl.BlockSpec(memory_space=pl.ANY)
PARAMS = pltpu.CompilerParams(vmem_limit_bytes=8 << 20)


def kept(array):
    return pltpu.with_memory_space_constraint(array, pltpu.VMEM)


def swapped(array, mask):
    size = lax.axis_size("team")
    return lax.ppermute(array, "team", [(i, i ^ mask) for i in range(size)])


def norm_pieces(x):
    wide = x.astype(F32)
    value = jnp.sum(wide * wide, axis=1, keepdims=True) * -0.125
    high = value.astype(BF16).astype(F32)
    rest = value - high
    middle = rest.astype(BF16).astype(F32)
    return high, middle, rest - middle


def norm_lanes(x, first):
    high, middle, low = norm_pieces(x)
    lane = lax.broadcasted_iota(jnp.int32, x.shape, 1)
    out = jnp.where(lane < 6, 1.0, 0.0)
    out = jnp.where(lane == first, high, out)
    out = jnp.where(lane == first + 1, middle, out)
    out = jnp.where(lane == first + 2, low, out)
    return out.astype(BF16)


def row_kernel(x_ref, rows_ref):
    x = x_ref[...]
    width = x.shape[1]
    rows_ref[:, :width] = x * jnp.asarray(0.25, BF16)
    rows_ref[:, width:] = norm_lanes(x, 3)


def first_tile(rows_ref, x_ref, e_ref, cols, row_block, before, after):
    n, width = x_ref.shape
    cols[:, :width] = x_ref[...]
    cols[:, width:] = norm_lanes(x_ref[...], 0)
    col_block = min(n, 256)
    for r in range(0, n, row_block):
        rows = slice(r, r + row_block)
        left = rows_ref[rows, :]
        total = before(rows)
        for c in range(0, n, col_block):
            part = slice(c, c + col_block)
            k = jnp.exp(lax.dot_general(left, cols[part, :], NT, preferred_element_type=F32))
            for l in range(0, col_block, 128):
                total = total + k[:, l : l + 128]
            e_ref[rows, part] = k * k
        after(rows, total)


def first_kernel(count, start, *refs):
    rows_ref, refs = refs[0], refs[1:]
    x_refs, refs = refs[:count], refs[count:]
    if start:
        acc_in = None
    else:
        acc_in, refs = refs[0], refs[1:]
    e_refs, refs = refs[:count], refs[count:]
    acc_ref, cols = refs
    row_block = min(256, rows_ref.shape[0])
    for j in range(count):
        if j:
            before = lambda rows: acc_ref[rows, :]
        elif start:
            before = lambda rows: jnp.zeros((row_block, 128), F32)
        else:
            before = lambda rows: acc_in[rows, :]

        def after(rows, total):
            acc_ref[rows, :] = total

        first_tile(rows_ref, x_refs[j], e_refs[j], cols, row_block, before, after)


def across(column):
    n = column.shape[0]
    wide = jnp.broadcast_to(column, (n, 128))
    row = lax.broadcasted_iota(jnp.int32, (n, 128), 0) % 128
    lane = lax.broadcasted_iota(jnp.int32, (n, 128), 1)
    return jnp.sum(jnp.where(row == lane, wide, 0.0).reshape(n // 128, 128, 128), axis=1)


def sums_kernel(acc_ref, sums_ref):
    sums_ref[...] = across(jnp.sum(acc_ref[...], axis=1, keepdims=True))


def pack_kernel(own_ref, mate_ref, both_ref):
    g = own_ref.shape[0]
    both_ref[:g, :] = own_ref[...]
    both_ref[g:, :] = mate_ref[...]


def weighted_tile(rows, e_ref, scale, x_ref, total, numerator):
    n = x_ref.shape[0]
    col_block = min(n, 256)
    for c in range(0, n, col_block):
        weights = []
        for l in range(c, c + col_block, 128):
            w = e_ref[rows, l : l + 128] * scale[l // 128 : l // 128 + 1, :]
            total = total + w
            weights.append(w.astype(BF16))
        weight = weights[0] if len(weights) == 1 else jnp.concatenate(weights, axis=1)
        numerator = numerator + jnp.dot(weight, x_ref[c : c + col_block, :], preferred_element_type=F32)
    return total, numerator


def second_kernel(points, count, *refs):
    e_refs, refs = refs[:count], refs[count:]
    s_refs, refs = refs[: count // 2], refs[count // 2 :]
    x_refs, refs = refs[:count], refs[count:]
    num_ref, acc_ref = refs
    n = x_refs[0].shape[0]
    groups = n // 128
    row_block = min(128, n)
    scales = [float(points) / s_refs[j // 2][(j % 2) * groups : (j % 2 + 1) * groups, :] for j in range(count)]
    for r in range(0, n, row_block):
        rows = slice(r, r + row_block)
        total = jnp.zeros((row_block, 128), F32)
        numerator = jnp.zeros((row_block, x_refs[0].shape[1]), F32)
        for j in range(count):
            total, numerator = weighted_tile(rows, e_refs[j], scales[j], x_refs[j], total, numerator)
        acc_ref[rows, :] = total
        num_ref[rows, :] = numerator


def last_kernel(points, count, *refs):
    e_refs, refs = refs[:count], refs[count:]
    s_refs, refs = refs[: count // 2], refs[count // 2 :]
    x_refs, refs = refs[:count], refs[count:]
    num_in, acc_in, own_ref, sums_ref, pot_hbm, out_hbm, pot_ref, out_ref, sems = refs
    n = own_ref.shape[0]
    groups = n // 128
    row_block = min(128, n)
    log_count = jnp.log(jnp.float32(points))
    scales = [float(points) / s_refs[j // 2][(j % 2) * groups : (j % 2 + 1) * groups, :] for j in range(count)]
    copies = []
    seconds = []
    for i, r in enumerate(range(0, n, row_block)):
        rows = slice(r, r + row_block)
        total, numerator = acc_in[rows, :], num_in[rows, :]
        for j in range(count):
            total, numerator = weighted_tile(rows, e_refs[j], scales[j], x_refs[j], total, numerator)
        second = jnp.sum(total, axis=1, keepdims=True)
        seconds.append(across(second))
        out_ref[rows, :] = own_ref[rows, :].astype(F32) - numerator / second
        copies.append(pltpu.make_async_copy(out_ref.at[rows, :], out_hbm.at[rows, :], sems.at[i]))
        copies[-1].start()
    second = jnp.concatenate(seconds, axis=0)
    pot_one = -2.0 * (jnp.log(sums_ref[...]) - log_count)
    pot_ref[...] = 0.5 * (pot_one - 2.0 * (jnp.log(second) - log_count))
    copies.append(pltpu.make_async_copy(pot_ref, pot_hbm, sems.at[len(copies)]))
    copies[-1].start()
    for copy in copies:
        copy.wait()


def shards(points):
    n, width = points.shape
    team = lax.axis_size("team")
    total_points = n * team
    groups = n // 128

    def tile(shape, dtype=F32):
        return pltpu.VMEM(shape, dtype)

    def call(kernel, out_shape, args, scratch=(), out_specs=None, name=None):
        single = not isinstance(out_shape, tuple)
        specs = out_specs or (IN_VMEM if single else tuple(IN_VMEM for _ in out_shape))
        return pl.pallas_call(
            kernel,
            out_shape=out_shape,
            in_specs=[IN_VMEM] * len(args),
            out_specs=specs,
            scratch_shapes=list(scratch),
            compiler_params=PARAMS,
            name=name,
        )(*[kept(a) for a in args])

    masks = list(range(2, team, 2))
    mate = swapped(points, 1)
    far = [swapped(points, m) for m in masks]
    pairs = [(points, mate)] + [(f, swapped(f, 1)) for f in far]

    rows = call(row_kernel, tile((n, 2 * width), BF16), [points], name="rows")
    tiles = []
    acc = None
    for pair in pairs:
        for x in pair:
            args = [rows, x] + ([] if acc is None else [acc])
            e, acc = call(
                functools.partial(first_kernel, 1, acc is None),
                (tile((n, n)), tile((n, 128))),
                args,
                scratch=[pltpu.VMEM((n, 2 * width), BF16)],
                name="first",
            )
            tiles.append(e)
    sums = call(sums_kernel, tile((groups, 128)), [acc], name="sums")
    mate_sums = swapped(sums, 1)
    both = call(pack_kernel, tile((2 * groups, 128)), [sums, mate_sums], name="pack")
    packs = [both] + [swapped(both, m) for m in masks]

    flat = [x for pair in pairs for x in pair]
    split = 4
    numerator, second = call(
        functools.partial(second_kernel, total_points, split),
        (tile((n, width)), tile((n, 128))),
        tiles[:split] + packs[: split // 2] + flat[:split],
        name="second",
    )
    count = len(flat) - split
    chunks = n // min(128, n)
    potential, displacement = call(
        functools.partial(last_kernel, total_points, count),
        (jax.ShapeDtypeStruct((groups, 128), F32), jax.ShapeDtypeStruct((n, width), F32)),
        tiles[split:] + packs[split // 2 :] + flat[split:] + [numerator, second, points, sums],
        scratch=[
            pltpu.VMEM((groups, 128), F32),
            pltpu.VMEM((n, width), F32),
            pltpu.SemaphoreType.DMA((chunks + 1,)),
        ],
        out_specs=(IN_HBM, IN_HBM),
        name="last",
    )
    return potential.reshape(n), displacement


def shifted(block, axis, distance):
    devices = range(lax.axis_size(axis))
    route = [((i - distance) % len(devices), i) for i in devices]
    return lax.ppermute(block, axis, route)


def square_norms(block_points):
    return jnp.sum(jnp.square(block_points.astype(jnp.float32)), axis=1)


def digit_set(offset, bit_index):
    return jnp.right_shift(offset, bit_index) % 2 == 1


def deliver_partner(block_points, offset):
    digits = lax.axis_size("rep").bit_length()
    current = block_points
    for bit_index in range(digits):
        arrived = shifted(current, "team", -(1 << bit_index))
        current = jnp.where(digit_set(offset, bit_index), arrived, current)
    return current


def deliver_mirror(block_points, offset):
    digits = lax.axis_size("rep").bit_length()
    current = block_points
    for bit_index in range(digits):
        arrived = shifted(current, "team", 1 << bit_index)
        current = jnp.where(digit_set(offset, bit_index), arrived, current)
    return current


def potential_partner(pot_one, offset):
    digits = lax.axis_size("rep").bit_length()
    current = pot_one
    for bit_index in range(digits):
        arrived = shifted(current, "team", -(1 << bit_index))
        current = jnp.where(digit_set(offset, bit_index), arrived, current)
    return current


def potential_mirror(pot_one, offset):
    digits = lax.axis_size("rep").bit_length()
    current = pot_one
    for bit_index in range(digits):
        arrived = shifted(current, "team", 1 << bit_index)
        current = jnp.where(digit_set(offset, bit_index), arrived, current)
    return current


def tile_sums(row_side, col_side, inv_eps, with_num):
    rows_x, rows_sq, rows_pot = row_side
    cols_x, cols_sq, cols_pot = col_side
    block_rows = rows_x.shape[0]
    numer_width = rows_x.shape[1] if with_num else 0
    col_count = 0
    row_block = min(block_rows, 512)
    col_block = min(block_rows, 256)
    cols_scale = jnp.exp(cols_pot * inv_eps)
    initial = (
        jnp.zeros((block_rows,), jnp.float32),
        jnp.zeros((block_rows, numer_width), jnp.float32),
        jnp.zeros((col_count,), jnp.float32),
        jnp.zeros((col_count, numer_width), jnp.float32),
    )

    def row_step(row_index, carried):
        row_total, row_numer, col_total, col_numer = carried
        row_start = row_index * row_block
        part_x = lax.dynamic_slice_in_dim(rows_x, row_start, row_block, 0)
        part_sq = lax.dynamic_slice_in_dim(rows_sq, row_start, row_block, 0)

        def col_step(col_index, inner_carried):
            block_total, block_numer, col_acc, col_num_acc = inner_carried
            col_start = col_index * col_block
            other_x = lax.dynamic_slice_in_dim(cols_x, col_start, col_block, 0)
            other_sq = lax.dynamic_slice_in_dim(cols_sq, col_start, col_block, 0)
            other_scale = lax.dynamic_slice_in_dim(cols_scale, col_start, col_block, 0)
            products = lax.dot_general(
                part_x, other_x, (((1,), (1,)), ((), ())), preferred_element_type=jnp.float32
            )
            kernel = jnp.exp(
                (products - 0.5 * part_sq[:, None] - 0.5 * other_sq[None, :]) * inv_eps
            )
            row_weight = kernel * other_scale[None, :]
            block_total = block_total + jnp.sum(row_weight, axis=1)
            if with_num:
                block_numer = block_numer + jnp.dot(
                    row_weight.astype(jnp.bfloat16), other_x, preferred_element_type=jnp.float32
                )
            return (block_total, block_numer, col_acc, col_num_acc)

        start_inner = (
            jnp.zeros((row_block,), jnp.float32),
            jnp.zeros((row_block, numer_width), jnp.float32),
            col_total,
            col_numer,
        )
        block_total, block_numer, col_total, col_numer = lax.fori_loop(
            0, block_rows // col_block, col_step, start_inner
        )
        row_total = lax.dynamic_update_slice_in_dim(row_total, block_total, row_start, 0)
        row_numer = lax.dynamic_update_slice_in_dim(row_numer, block_numer, row_start, 0)
        return (row_total, row_numer, col_total, col_numer)

    return lax.fori_loop(0, block_rows // row_block, row_step, initial)


def crossed_sums(own_side, partner_side, mirror_side, inv_eps, with_num):
    forward_part = tile_sums(own_side, partner_side, inv_eps, with_num)
    backward_part = tile_sums(own_side, mirror_side, inv_eps, with_num)
    return (forward_part[0] + backward_part[0], forward_part[1] + backward_part[1])


def neighbour_potentials(pot_one, offset, replica):
    partner_pot = potential_partner(pot_one, offset)
    mirror_pot = potential_mirror(pot_one, offset)
    mirror_pot = jnp.where(replica == 0, pot_one, mirror_pot)
    return (partner_pot, mirror_pot)


def looped_shards(points):
    block_rows = points.shape[0]
    replicas = lax.axis_size("rep")
    team_count = lax.axis_size("team")
    replica = lax.axis_index("rep")
    offset = jnp.where(replica == 0, replicas, replica)
    own_sq = square_norms(points)
    log_count = jnp.log(jnp.float32(block_rows * team_count))
    zero_pot = jnp.zeros((block_rows,), jnp.float32)
    partner_x = deliver_partner(points, offset)
    partner_sq = square_norms(partner_x)
    mirror_far = deliver_mirror(points, offset)
    mirror_x = jnp.where(replica == 0, points, mirror_far)
    mirror_sq = square_norms(mirror_x)
    first_local, unused_numer = crossed_sums(
        (points, own_sq, zero_pot),
        (partner_x, partner_sq, zero_pot),
        (mirror_x, mirror_sq, zero_pot),
        0.25,
        False,
    )
    first_sum = lax.psum(first_local, "rep")
    pot_one = 0.5 * (zero_pot - 4.0 * (jnp.log(first_sum) - log_count))
    partner_pot, mirror_pot = neighbour_potentials(pot_one, offset, replica)
    second_local, numer_local = crossed_sums(
        (points, own_sq, pot_one),
        (partner_x, partner_sq, partner_pot),
        (mirror_x, mirror_sq, mirror_pot),
        0.5,
        True,
    )
    second, numerator = lax.psum((second_local, numer_local), "rep")
    potential = 0.5 * (pot_one - 2.0 * (jnp.log(second) - log_count))
    displacement = points.astype(jnp.float32) - numerator / second[:, None]
    return (potential, displacement)


TILE_BYTES = 36 << 20


def solution(mesh):
    team = mesh.shape["team"]

    def body(points):
        n = points.shape[0]
        fits = 4 * n * n * team <= TILE_BYTES and team == 8 and n % 256 == 0
        return shards(points) if fits else looped_shards(points)

    return jax.shard_map(
        body,
        mesh=mesh,
        in_specs=(P("team", None),),
        out_specs=(P("team"), P("team", None)),
        check_vma=False,
    )
```

```python
import functools
import jax
import jax.numpy as jnp
from jax import lax
from jax.experimental import pallas as pl
from jax.experimental.pallas import tpu as pltpu
from jax.sharding import PartitionSpec as P

F32 = jnp.float32
BF16 = jnp.bfloat16
NT = (((1,), (1,)), ((), ()))
IN_VMEM = pl.BlockSpec(memory_space=pltpu.VMEM)
IN_HBM = pl.BlockSpec(memory_space=pl.ANY)
PARAMS = pltpu.CompilerParams(vmem_limit_bytes=16 << 20)


def kept(array):
    return pltpu.with_memory_space_constraint(array, pltpu.VMEM)


def swapped(array, mask):
    size = lax.axis_size("team")
    return lax.ppermute(array, "team", [(i, i ^ mask) for i in range(size)])


def exchanged(array, even, odd):
    size = lax.axis_size("team")
    return lax.ppermute(array, "team", [(i, i ^ (odd if i % 2 else even)) for i in range(size)])


def down(rows):
    row = lax.broadcasted_iota(jnp.int32, (128, 128), 0)
    diagonal = row == lax.broadcasted_iota(jnp.int32, (128, 128), 1)
    wide = [jnp.where(diagonal, rows[g : g + 1, :], 0.0) for g in range(rows.shape[0])]
    return jnp.concatenate([jnp.broadcast_to(jnp.sum(w, axis=1, keepdims=True), (128, 128)) for w in wide], axis=0)


def across(columns):
    row = lax.broadcasted_iota(jnp.int32, (128, 128), 0)
    diagonal = row == lax.broadcasted_iota(jnp.int32, (128, 128), 1)
    sums = [jnp.sum(columns[g : g + 128, :], axis=1, keepdims=True) for g in range(0, columns.shape[0], 128)]
    return [jnp.sum(jnp.where(diagonal, s, 0.0), axis=0, keepdims=True) for s in sums]


def pieces(x_turned):
    wide = x_turned.astype(F32)
    norms = jnp.sum(wide * wide, axis=0, keepdims=True)
    high = norms.astype(BF16).astype(F32)
    rest = norms - high
    middle = rest.astype(BF16).astype(F32)
    return high, middle, rest - middle


def put_columns(cols, part, x, x_turned):
    width = x.shape[1]
    high, middle, low = pieces(x_turned)
    sub = lax.broadcasted_iota(jnp.int32, (16, x.shape[0]), 0)
    extra = jnp.where(sub == 0, high, jnp.where(sub == 1, middle, jnp.where(sub == 2, low, 1.0))).astype(BF16)
    cols[part, :width] = x
    cols[part, width:] = jnp.concatenate([extra] * (width // 16), axis=0).T


def put_rows(rows, x_turned):
    width, n = x_turned.shape
    high, middle, low = pieces(x_turned)
    sub = lax.broadcasted_iota(jnp.int32, (16, n), 0)
    norm = jnp.where(sub == 3, high, jnp.where(sub == 4, middle, low))
    extra = jnp.where(sub < 3, -0.125, jnp.where(sub < 6, norm * -0.125, 0.0))
    rows[:width, :] = x_turned * jnp.asarray(0.25, BF16)
    rows[width : width + 16, :] = extra.astype(BF16)
    rows[width + 16 :, :] = jnp.zeros((width - 16, n), BF16)


def row_kernel(x_ref, rows_ref, own_ref):
    own_ref[...] = x_ref[...]
    put_rows(rows_ref, x_ref[...].T)


def first_kernel(count, start, sums, *refs):
    rows_ref, x_refs, refs = refs[0], refs[1 : 1 + count], refs[1 + count :]
    if sums and not start:
        acc_in, refs = refs[0], refs[1:]
    e_refs, turned_refs, refs = refs[:count], refs[count : 2 * count], refs[2 * count :]
    if sums:
        acc_ref, refs = refs[0], refs[1:]
    n = x_refs[0].shape[0]
    block = 256
    for i in range(0, n, block):
        groups = range(i // 128, (i + block) // 128)
        if sums:
            totals = [jnp.zeros((8, 128), F32) if start else acc_in[8 * g : 8 * g + 8, :] for g in groups]
        for x_ref, e_ref, turned_ref, cols in zip(x_refs, e_refs, turned_refs, refs):
            for j in range(0, n, block):
                part = slice(j, j + block)
                if i == 0:
                    x_turned = x_ref[part, :].T
                    turned_ref[:, part] = x_turned
                    put_columns(cols, part, x_ref[part, :], x_turned)
                p = jnp.dot(cols[part, :], rows_ref[:, i : i + block], preferred_element_type=F32)
                for t, g in enumerate(groups):
                    k = jnp.exp(p[:, t * 128 : (t + 1) * 128])
                    e_ref[part, g * 128 : g * 128 + 128] = k * k
                    if sums:
                        totals[t] = totals[t] + jnp.sum(k.reshape(block // 8, 8, 128), axis=0)
        if sums:
            for t, g in enumerate(groups):
                acc_ref[8 * g : 8 * g + 8, :] = totals[t]


def between_kernel(near_ref, cross_ref, near_mate_ref, cross_mate_ref, near_t, cross_t, acc_in, out_ref, rows, cols, x, row_sums):
    me = lax.axis_index("team")
    core, side = me % 2, (me // 2) % 2
    n, width = near_ref.shape
    groups = n // 128
    block = 256

    @pl.when(core == 0)
    def _():
        rows[:width, :] = near_t[...]

    @pl.when(core == 1)
    def _():
        rows[:width, :] = cross_t[...]

    for which, (c, s) in ((cross_ref, (0, 0)), (near_ref, (1, 0)), (near_mate_ref, (0, 1)), (cross_mate_ref, (1, 1))):

        @pl.when((core == c) & (side == s))
        def _(which=which):
            x[...] = which[...]

    put_rows(rows, rows[:width, :])
    for j in range(0, n, block):
        part = slice(j, j + block)
        put_columns(cols, part, x[part, :], x[part, :].T)
        row_sums[part, :] = jnp.zeros((block, 128), F32)
    for g in range(groups):
        out_ref[g : g + 1, :] = jnp.sum(acc_in[8 * g : 8 * g + 8, :], axis=0, keepdims=True)
    for i in range(0, n, block):
        totals = [jnp.zeros((8, 128), F32) for _ in range(block // 128)]
        for j in range(0, n, block):
            part = slice(j, j + block)
            p = jnp.dot(cols[part, :], rows[:, i : i + block], preferred_element_type=F32)
            along = row_sums[part, :]
            for t in range(block // 128):
                k = jnp.exp(p[:, t * 128 : (t + 1) * 128])
                along = along + k
                totals[t] = totals[t] + jnp.sum(k.reshape(block // 8, 8, 128), axis=0)
            row_sums[part, :] = along
        for t, total in enumerate(totals):
            g = groups + i // 128 + t
            out_ref[g : g + 1, :] = jnp.sum(total, axis=0, keepdims=True)
    other = jnp.concatenate(across(row_sums[...]), axis=0)
    zero = jnp.zeros_like(other)
    out_ref[2 * groups : 3 * groups, :] = jnp.where(side == 0, other, zero)
    out_ref[3 * groups :, :] = jnp.where(side == 1, other, zero)


def pack_kernel(own_ref, mate_ref, both_ref):
    g = own_ref.shape[0]
    both_ref[:g, :] = own_ref[...]
    both_ref[g:, :] = mate_ref[...]


def second_kernel(points, masks, *refs):
    count = len(masks)
    e_refs, refs = refs[:count], refs[count:]
    x_refs, refs = refs[:count], refs[count:]
    packs, refs = refs[: count // 2], refs[count // 2 :]
    own_ref, pot_hbm, out_hbm, scales, pot_ref, out_ref, sems = refs
    width, n = x_refs[0].shape
    groups = n // 128
    block = 256
    core = lax.axis_index("team") % 2

    def message(mask, slot):
        first = (mask % 2 * 4 + slot) * groups
        return packs[(0, 2, 3, 1)[mask // 2]][first : first + groups, :]

    def first_sum(mask):
        near = message(mask ^ 2, 1) + message(mask ^ 4, 2)
        return message(mask, 0) + near + message(mask ^ 5, 3)

    def put_scales(t):
        even, odd = masks[t]
        total = first_sum(even) if even == odd else jnp.where(core == 0, first_sum(even), first_sum(odd))
        scales[t * n : (t + 1) * n, :] = down(float(points) / total)

    copies = []
    seconds = []
    for i in range(0, n, block):
        lanes = range(i, i + block, 128)
        cols = slice(i, i + block)
        numerator = jnp.zeros((width, block), F32)
        totals = [jnp.zeros((8, 128), F32) for _ in lanes]
        for t in range(count):
            if i == 0:
                put_scales(t)
            for j in range(0, n, block):
                scale = scales[t * n + j : t * n + j + block, :]
                weights = []
                for u, l in enumerate(lanes):
                    w = e_refs[t][j : j + block, l : l + 128] * scale
                    totals[u] = totals[u] + jnp.sum(w.reshape(block // 8, 8, 128), axis=0)
                    weights.append(w.astype(BF16))
                weight = jnp.concatenate(weights, axis=1)
                numerator = numerator + jnp.dot(x_refs[t][:, j : j + block], weight, preferred_element_type=F32)
        for u, l in enumerate(lanes):
            second = jnp.sum(totals[u], axis=0, keepdims=True)
            seconds.append(second)
            image = (numerator[:, u * 128 : (u + 1) * 128] / second).T
            out_ref[l : l + 128, :] = own_ref[l : l + 128, :].astype(F32) - image
        copies.append(pltpu.make_async_copy(out_ref.at[cols, :], out_hbm.at[cols, :], sems.at[len(copies)]))
        copies[-1].start()
    log_count = jnp.log(jnp.float32(points))
    second = jnp.concatenate(seconds, axis=0)
    pot_one = -2.0 * (jnp.log(first_sum(0)) - log_count)
    pot_ref[...] = 0.5 * (pot_one - 2.0 * (jnp.log(second) - log_count))
    copies.append(pltpu.make_async_copy(pot_ref, pot_hbm, sems.at[len(copies)]))
    copies[-1].start()
    for copy in copies:
        copy.wait()


def shards(points):
    n, width = points.shape
    total_points = n * lax.axis_size("team")
    groups = n // 128
    chunks = n // 256

    def tile(shape, dtype=F32):
        return pltpu.VMEM(shape, dtype)

    def call(kernel, out_shape, args, scratch=(), out_specs=None, name=None, tiles=0):
        single = not isinstance(out_shape, tuple)
        specs = out_specs or (IN_VMEM if single else tuple(IN_VMEM for _ in out_shape))
        return pl.pallas_call(
            kernel,
            out_shape=out_shape,
            in_specs=[IN_VMEM] * len(args),
            out_specs=specs,
            scratch_shapes=list(scratch),
            compiler_params=PARAMS,
            cost_estimate=pl.CostEstimate(flops=tiles * 24 * n * n * width, bytes_accessed=0, transcendentals=0),
            name=name,
        )(*[kept(a) for a in args])

    acc = None
    done = {}

    def first(blocks, sums=True):
        nonlocal acc
        count = len(blocks)
        out = call(
            functools.partial(first_kernel, count, acc is None, sums),
            (tile((n, n)),) * count + (tile((width, n), BF16),) * count + (tile((8 * groups, 128)),) * sums,
            [rows, *blocks.values()] + ([acc] if sums and acc is not None else []),
            scratch=[pltpu.VMEM((n, 2 * width), BF16)] * count,
            name="first",
            tiles=count,
        )
        for t, block in enumerate(blocks):
            done[block] = (out[t], out[count + t])
        if sums:
            acc = out[-1]

    def after(x):
        nonlocal acc
        x, acc = lax.optimization_barrier((x, acc))
        return x

    near = exchanged(points, 2, 4)
    mate = swapped(points, 1)
    rows, own = call(row_kernel, (tile((2 * width, n), BF16), tile((n, width), BF16)), [points], name="rows")
    first(dict(own=own))
    cross = exchanged(after(points), 4, 2)
    first(dict(mate=mate))
    near = after(near)
    near_mate = swapped(near, 1)
    first(dict(near=near))
    diagonal = exchanged(after(near), 4, 2)
    cross_mate = swapped(cross, 1)
    first(dict(cross=cross))
    first(dict(near_mate=near_mate, cross_mate=cross_mate))
    sums = call(
        between_kernel,
        tile((4 * groups, 128)),
        [near, cross, near_mate, cross_mate, done["near"][1], done["cross"][1], acc],
        scratch=[
            pltpu.VMEM((2 * width, n), BF16),
            pltpu.VMEM((n, 2 * width), BF16),
            pltpu.VMEM((n, width), BF16),
            pltpu.VMEM((n, 128), F32),
        ],
        name="between",
        tiles=1,
    )
    mate_sums = swapped(sums, 1)
    both = call(pack_kernel, tile((8 * groups, 128)), [sums, mate_sums], name="pack")
    far, *packs = [swapped(both, m) for m in (6, 2, 4)]
    packs = [both, far, *packs]
    diagonal, both = lax.optimization_barrier((diagonal, both))
    diagonal_mate = swapped(diagonal, 1)
    first(dict(diagonal=diagonal), sums=False)
    first(dict(diagonal_mate=diagonal_mate), sums=False)
    masks = dict(
        own=(0, 0),
        mate=(1, 1),
        near=(2, 4),
        cross_mate=(3, 5),
        cross=(4, 2),
        near_mate=(5, 3),
        diagonal=(6, 6),
        diagonal_mate=(7, 7),
    )
    potential, displacement = call(
        functools.partial(second_kernel, total_points, list(masks.values())),
        (jax.ShapeDtypeStruct((groups, 128), F32), jax.ShapeDtypeStruct((n, width), F32)),
        [done[b][0] for b in masks] + [done[b][1] for b in masks] + packs + [own],
        scratch=[
            pltpu.VMEM((len(masks) * n, 128), F32),
            pltpu.VMEM((groups, 128), F32),
            pltpu.VMEM((n, width), F32),
            pltpu.SemaphoreType.DMA((chunks + 1,)),
        ],
        out_specs=(IN_HBM, IN_HBM),
        name="second",
        tiles=len(masks),
    )
    return potential.reshape(n), displacement


def shifted(block, axis, distance):
    devices = range(lax.axis_size(axis))
    route = [((i - distance) % len(devices), i) for i in devices]
    return lax.ppermute(block, axis, route)


def square_norms(block_points):
    return jnp.sum(jnp.square(block_points.astype(jnp.float32)), axis=1)


def digit_set(offset, bit_index):
    return jnp.right_shift(offset, bit_index) % 2 == 1


def deliver_partner(block_points, offset):
    digits = lax.axis_size("rep").bit_length()
    current = block_points
    for bit_index in range(digits):
        arrived = shifted(current, "team", -(1 << bit_index))
        current = jnp.where(digit_set(offset, bit_index), arrived, current)
    return current


def deliver_mirror(block_points, offset):
    digits = lax.axis_size("rep").bit_length()
    current = block_points
    for bit_index in range(digits):
        arrived = shifted(current, "team", 1 << bit_index)
        current = jnp.where(digit_set(offset, bit_index), arrived, current)
    return current


def potential_partner(pot_one, offset):
    digits = lax.axis_size("rep").bit_length()
    current = pot_one
    for bit_index in range(digits):
        arrived = shifted(current, "team", -(1 << bit_index))
        current = jnp.where(digit_set(offset, bit_index), arrived, current)
    return current


def potential_mirror(pot_one, offset):
    digits = lax.axis_size("rep").bit_length()
    current = pot_one
    for bit_index in range(digits):
        arrived = shifted(current, "team", 1 << bit_index)
        current = jnp.where(digit_set(offset, bit_index), arrived, current)
    return current


def tile_sums(row_side, col_side, inv_eps, with_num):
    rows_x, rows_sq, rows_pot = row_side
    cols_x, cols_sq, cols_pot = col_side
    block_rows = rows_x.shape[0]
    numer_width = rows_x.shape[1] if with_num else 0
    col_count = 0
    row_block = min(block_rows, 512)
    col_block = min(block_rows, 256)
    cols_scale = jnp.exp(cols_pot * inv_eps)
    initial = (
        jnp.zeros((block_rows,), jnp.float32),
        jnp.zeros((block_rows, numer_width), jnp.float32),
        jnp.zeros((col_count,), jnp.float32),
        jnp.zeros((col_count, numer_width), jnp.float32),
    )

    def row_step(row_index, carried):
        row_total, row_numer, col_total, col_numer = carried
        row_start = row_index * row_block
        part_x = lax.dynamic_slice_in_dim(rows_x, row_start, row_block, 0)
        part_sq = lax.dynamic_slice_in_dim(rows_sq, row_start, row_block, 0)

        def col_step(col_index, inner_carried):
            block_total, block_numer, col_acc, col_num_acc = inner_carried
            col_start = col_index * col_block
            other_x = lax.dynamic_slice_in_dim(cols_x, col_start, col_block, 0)
            other_sq = lax.dynamic_slice_in_dim(cols_sq, col_start, col_block, 0)
            other_scale = lax.dynamic_slice_in_dim(cols_scale, col_start, col_block, 0)
            products = lax.dot_general(
                part_x, other_x, (((1,), (1,)), ((), ())), preferred_element_type=jnp.float32
            )
            kernel = jnp.exp(
                (products - 0.5 * part_sq[:, None] - 0.5 * other_sq[None, :]) * inv_eps
            )
            row_weight = kernel * other_scale[None, :]
            block_total = block_total + jnp.sum(row_weight, axis=1)
            if with_num:
                block_numer = block_numer + jnp.dot(
                    row_weight.astype(jnp.bfloat16), other_x, preferred_element_type=jnp.float32
                )
            return (block_total, block_numer, col_acc, col_num_acc)

        start_inner = (
            jnp.zeros((row_block,), jnp.float32),
            jnp.zeros((row_block, numer_width), jnp.float32),
            col_total,
            col_numer,
        )
        block_total, block_numer, col_total, col_numer = lax.fori_loop(
            0, block_rows // col_block, col_step, start_inner
        )
        row_total = lax.dynamic_update_slice_in_dim(row_total, block_total, row_start, 0)
        row_numer = lax.dynamic_update_slice_in_dim(row_numer, block_numer, row_start, 0)
        return (row_total, row_numer, col_total, col_numer)

    return lax.fori_loop(0, block_rows // row_block, row_step, initial)


def crossed_sums(own_side, partner_side, mirror_side, inv_eps, with_num):
    forward_part = tile_sums(own_side, partner_side, inv_eps, with_num)
    backward_part = tile_sums(own_side, mirror_side, inv_eps, with_num)
    return (forward_part[0] + backward_part[0], forward_part[1] + backward_part[1])


def neighbour_potentials(pot_one, offset, replica):
    partner_pot = potential_partner(pot_one, offset)
    mirror_pot = potential_mirror(pot_one, offset)
    mirror_pot = jnp.where(replica == 0, pot_one, mirror_pot)
    return (partner_pot, mirror_pot)


def looped_shards(points):
    block_rows = points.shape[0]
    replicas = lax.axis_size("rep")
    team_count = lax.axis_size("team")
    replica = lax.axis_index("rep")
    offset = jnp.where(replica == 0, replicas, replica)
    own_sq = square_norms(points)
    log_count = jnp.log(jnp.float32(block_rows * team_count))
    zero_pot = jnp.zeros((block_rows,), jnp.float32)
    partner_x = deliver_partner(points, offset)
    partner_sq = square_norms(partner_x)
    mirror_far = deliver_mirror(points, offset)
    mirror_x = jnp.where(replica == 0, points, mirror_far)
    mirror_sq = square_norms(mirror_x)
    first_local, unused_numer = crossed_sums(
        (points, own_sq, zero_pot),
        (partner_x, partner_sq, zero_pot),
        (mirror_x, mirror_sq, zero_pot),
        0.25,
        False,
    )
    first_sum = lax.psum(first_local, "rep")
    pot_one = 0.5 * (zero_pot - 4.0 * (jnp.log(first_sum) - log_count))
    partner_pot, mirror_pot = neighbour_potentials(pot_one, offset, replica)
    second_local, numer_local = crossed_sums(
        (points, own_sq, pot_one),
        (partner_x, partner_sq, partner_pot),
        (mirror_x, mirror_sq, mirror_pot),
        0.5,
        True,
    )
    second, numerator = lax.psum((second_local, numer_local), "rep")
    potential = 0.5 * (pot_one - 2.0 * (jnp.log(second) - log_count))
    displacement = points.astype(jnp.float32) - numerator / second[:, None]
    return (potential, displacement)


TILE_BYTES = 36 << 20


def solution(mesh):
    team = mesh.shape["team"]

    def body(points):
        n = points.shape[0]
        fits = 4 * n * n * team <= TILE_BYTES and team == 8 and n % 256 == 0
        return shards(points) if fits else looped_shards(points)

    return jax.shard_map(
        body,
        mesh=mesh,
        in_specs=(P("team", None),),
        out_specs=(P("team"), P("team", None)),
        check_vma=False,
    )
```

```python
import functools
import jax
import jax.numpy as jnp
from jax import lax
from jax.experimental import pallas as pl
from jax.experimental.pallas import tpu as pltpu
from jax.sharding import PartitionSpec as P

F32 = jnp.float32
BF16 = jnp.bfloat16
NT = (((1,), (1,)), ((), ()))
IN_VMEM = pl.BlockSpec(memory_space=pltpu.VMEM)
IN_HBM = pl.BlockSpec(memory_space=pl.ANY)
PARAMS = pltpu.CompilerParams(vmem_limit_bytes=16 << 20)


def kept(array):
    return pltpu.with_memory_space_constraint(array, pltpu.VMEM)


def swapped(array, mask):
    size = lax.axis_size("team")
    return lax.ppermute(array, "team", [(i, i ^ mask) for i in range(size)])


def exchanged(array, even, odd):
    size = lax.axis_size("team")
    return lax.ppermute(array, "team", [(i, i ^ (odd if i % 2 else even)) for i in range(size)])


def across(columns):
    row = lax.broadcasted_iota(jnp.int32, (128, 128), 0)
    diagonal = row == lax.broadcasted_iota(jnp.int32, (128, 128), 1)
    sums = [jnp.sum(columns[g : g + 128, :], axis=1, keepdims=True) for g in range(0, columns.shape[0], 128)]
    return [jnp.sum(jnp.where(diagonal, s, 0.0), axis=0, keepdims=True) for s in sums]


def pieces(x_turned):
    wide = x_turned.astype(F32)
    norms = jnp.sum(wide * wide, axis=0, keepdims=True)
    high = norms.astype(BF16).astype(F32)
    rest = norms - high
    middle = rest.astype(BF16).astype(F32)
    return high, middle, rest - middle


def put_columns(cols, part, x, x_turned):
    width = x.shape[1]
    high, middle, low = pieces(x_turned)
    sub = lax.broadcasted_iota(jnp.int32, (16, x.shape[0]), 0)
    extra = jnp.where(sub == 0, high, jnp.where(sub == 1, middle, jnp.where(sub == 2, low, 1.0))).astype(BF16)
    cols[part, :width] = x
    cols[part, width:] = jnp.concatenate([extra] * (width // 16), axis=0).T


def put_rows(rows, x_turned):
    width, n = x_turned.shape
    high, middle, low = pieces(x_turned)
    sub = lax.broadcasted_iota(jnp.int32, (16, n), 0)
    norm = jnp.where(sub == 3, high, jnp.where(sub == 4, middle, low))
    extra = jnp.where(sub < 3, -0.125, jnp.where(sub < 6, norm * -0.125, 0.0))
    rows[:width, :] = x_turned * jnp.asarray(0.25, BF16)
    rows[width : width + 16, :] = extra.astype(BF16)
    rows[width + 16 :, :] = jnp.zeros((width - 16, n), BF16)


def row_kernel(x_ref, rows_ref, own_ref):
    own_ref[...] = x_ref[...]
    put_rows(rows_ref, x_ref[...].T)


def put_tiles(rows_ref, x_refs, e_refs, turned_refs, col_refs, acc_in, acc_ref):
    n = x_refs[0].shape[0]
    block = 256
    for i in range(0, n, block):
        groups = range(i // 128, (i + block) // 128)
        if acc_ref is not None:
            totals = [jnp.zeros((8, 128), F32) if acc_in is None else acc_in[8 * g : 8 * g + 8, :] for g in groups]
        for x_ref, e_ref, turned_ref, cols in zip(x_refs, e_refs, turned_refs, col_refs):
            for j in range(0, n, block):
                part = slice(j, j + block)
                if i == 0:
                    x_turned = x_ref[part, :].T
                    turned_ref[:, part] = x_turned
                    put_columns(cols, part, x_ref[part, :], x_turned)
                p = jnp.dot(cols[part, :], rows_ref[:, i : i + block], preferred_element_type=F32)
                for t, g in enumerate(groups):
                    k = jnp.exp(p[:, t * 128 : (t + 1) * 128])
                    e_ref[part, g * 128 : g * 128 + 128] = k * k
                    if acc_ref is not None:
                        totals[t] = totals[t] + jnp.sum(k.reshape(block // 8, 8, 128), axis=0)
        if acc_ref is not None:
            for t, g in enumerate(groups):
                acc_ref[8 * g : 8 * g + 8, :] = totals[t]


def first_kernel(count, start, sums, *refs):
    rows_ref, x_refs, refs = refs[0], refs[1 : 1 + count], refs[1 + count :]
    acc_in = acc_ref = None
    if sums and not start:
        acc_in, refs = refs[0], refs[1:]
    e_refs, turned_refs, refs = refs[:count], refs[count : 2 * count], refs[2 * count :]
    if sums:
        acc_ref, refs = refs[0], refs[1:]
    put_tiles(rows_ref, x_refs, e_refs, turned_refs, refs, acc_in, acc_ref)


def between_kernel(*refs):
    own_rows, near_ref, cross_ref, near_mate_ref, cross_mate_ref, near_t, cross_t, acc_in, *refs = refs
    e_ref, turned_ref, out_ref, rows, own_cols, cols, x, row_sums, acc = refs
    me = lax.axis_index("team")
    core, side = me % 2, (me // 2) % 2
    n, width = near_ref.shape
    groups = n // 128
    block = 256

    @pl.when(core == 0)
    def _():
        rows[:width, :] = near_t[...]

    @pl.when(core == 1)
    def _():
        rows[:width, :] = cross_t[...]

    for which, (c, s) in ((cross_ref, (0, 0)), (near_ref, (1, 0)), (near_mate_ref, (0, 1)), (cross_mate_ref, (1, 1))):

        @pl.when((core == c) & (side == s))
        def _(which=which):
            x[...] = which[...]

    put_rows(rows, rows[:width, :])
    for j in range(0, n, block):
        part = slice(j, j + block)
        put_columns(cols, part, x[part, :], x[part, :].T)
        row_sums[part, :] = jnp.zeros((block, 128), F32)
    put_tiles(own_rows, [cross_mate_ref], [e_ref], [turned_ref], [own_cols], acc_in, acc)
    for g in range(groups):
        out_ref[g : g + 1, :] = jnp.sum(acc[8 * g : 8 * g + 8, :], axis=0, keepdims=True)
    for i in range(0, n, block):
        totals = [jnp.zeros((8, 128), F32) for _ in range(block // 128)]
        for j in range(0, n, block):
            part = slice(j, j + block)
            p = jnp.dot(cols[part, :], rows[:, i : i + block], preferred_element_type=F32)
            along = row_sums[part, :]
            for t in range(block // 128):
                k = jnp.exp(p[:, t * 128 : (t + 1) * 128])
                along = along + k
                totals[t] = totals[t] + jnp.sum(k.reshape(block // 8, 8, 128), axis=0)
            row_sums[part, :] = along
        for t, total in enumerate(totals):
            g = groups + i // 128 + t
            out_ref[g : g + 1, :] = jnp.sum(total, axis=0, keepdims=True)
    out_ref[2 * groups :, :] = jnp.concatenate(across(row_sums[...]), axis=0)


def pack_kernel(*refs):
    step = refs[0].shape[0]
    for t, ref in enumerate(refs[:-1]):
        refs[-1][t * step : (t + 1) * step, :] = ref[...]


PARTS = (((0,), (1, 2)), ((1, 2), (3, 4, 5)), ((3, 4, 5), (6, 7)), ((6, 7), ()))


def second_kernel(points, masks, *refs):
    count = len(masks)
    e_refs, refs = refs[:count], refs[count:]
    x_refs, refs = refs[:count], refs[count:]
    pack_refs, refs = refs[:4], refs[4:]
    own_ref, pot_hbm, out_hbm, shares_ref, scales, num_ref, acc_ref, pot_ref, out_ref, sems = refs
    width, n = x_refs[0].shape
    groups = n // 128
    block = 256
    team = lax.axis_index("team")
    core, side = team % 2, team // 2 % 2

    def message(mask, slot):
        first = (mask % 2 * 3 + slot) * groups
        return pack_refs[(3, 1, 2, 0)[mask // 2]][first : first + groups, :]

    def first_sum(mask):
        near = message(mask, 0) + message(mask ^ 2, 1)
        return near + jnp.where(side == mask // 2 % 2, message(mask ^ 4, 2), message(mask ^ 5, 2))

    sums = [first_sum(mask) for mask in range(count)]
    order = [sums[even] if even == odd else jnp.where(core == 0, sums[even], sums[odd]) for even, odd in masks]
    shares = float(points) / jnp.concatenate(order, axis=0)
    shares_ref[...] = jnp.concatenate([shares, jnp.zeros((128 - count * groups, 128), F32)], axis=0).T

    def put_scales(t):
        for g in range(groups):
            first = t * n + g * 128
            lane = t * groups + g
            scales[first : first + 128, :] = jnp.broadcast_to(shares_ref[:, lane : lane + 1], (128, 128))

    def part(tiles, ahead):
        start = tiles[0] == 0
        for t in ahead:
            put_scales(t)
        for i in range(0, n, block):
            cols = slice(i, i + block)
            lanes = range(i, i + block, 128)
            numerator = jnp.zeros((width, block), F32) if start else num_ref[:, cols]
            totals = [jnp.zeros((8, 128), F32) if start else acc_ref[l // 16 : l // 16 + 8, :] for l in lanes]
            for t in tiles:
                for j in range(0, n, block):
                    scale = scales[t * n + j : t * n + j + block, :]
                    weights = []
                    for u, l in enumerate(lanes):
                        w = e_refs[t][j : j + block, l : l + 128] * scale
                        totals[u] = totals[u] + jnp.sum(w.reshape(block // 8, 8, 128), axis=0)
                        weights.append(w.astype(BF16))
                    weight = jnp.concatenate(weights, axis=1)
                    numerator = numerator + jnp.dot(x_refs[t][:, j : j + block], weight, preferred_element_type=F32)
            for u, l in enumerate(lanes):
                acc_ref[l // 16 : l // 16 + 8, :] = totals[u]
            num_ref[:, cols] = numerator

    def out_copy(i):
        rows = slice(i * block, (i + 1) * block)
        return pltpu.make_async_copy(out_ref.at[rows, :], out_hbm.at[rows, :], sems.at[i])

    put_scales(0)
    for tiles, ahead in PARTS:
        pl.when(team >= 0)(functools.partial(part, tiles, ahead))
    seconds = []
    for g in range(groups):
        rows = slice(g * 128, (g + 1) * 128)
        seconds.append(jnp.sum(acc_ref[8 * g : 8 * g + 8, :], axis=0, keepdims=True))
        out_ref[rows, :] = own_ref[rows, :].astype(F32) - (num_ref[:, rows] / seconds[-1]).T
        if (g + 1) * 128 % block == 0:
            out_copy(g * 128 // block).start()
    log_count = jnp.log(jnp.float32(points))
    second = jnp.concatenate(seconds, axis=0)
    pot_one = -2.0 * (jnp.log(sums[0]) - log_count)
    pot_ref[...] = 0.5 * (pot_one - 2.0 * (jnp.log(second) - log_count))
    pot_copy = pltpu.make_async_copy(pot_ref, pot_hbm, sems.at[n // block])
    pot_copy.start()
    for i in range(n // block):
        out_copy(i).wait()
    pot_copy.wait()


def shards(points):
    n, width = points.shape
    total_points = n * lax.axis_size("team")
    groups = n // 128
    chunks = n // 256

    def tile(shape, dtype=F32):
        return pltpu.VMEM(shape, dtype)

    def call(kernel, out_shape, args, scratch=(), out_specs=None, name=None, tiles=0):
        single = not isinstance(out_shape, tuple)
        specs = out_specs or (IN_VMEM if single else tuple(IN_VMEM for _ in out_shape))
        return pl.pallas_call(
            kernel,
            out_shape=out_shape,
            in_specs=[IN_VMEM] * len(args),
            out_specs=specs,
            scratch_shapes=list(scratch),
            compiler_params=PARAMS,
            cost_estimate=pl.CostEstimate(flops=tiles * 24 * n * n * width, bytes_accessed=0, transcendentals=0),
            name=name,
        )(*[kept(a) for a in args])

    acc = None
    done = {}

    def first(blocks, sums=True):
        nonlocal acc
        count = len(blocks)
        out = call(
            functools.partial(first_kernel, count, acc is None, sums),
            (tile((n, n)),) * count + (tile((width, n), BF16),) * count + (tile((8 * groups, 128)),) * sums,
            [rows, *blocks.values()] + ([acc] if sums and acc is not None else []),
            scratch=[pltpu.VMEM((n, 2 * width), BF16)] * count,
            name="first",
            tiles=count,
        )
        for t, block in enumerate(blocks):
            done[block] = (out[t], out[count + t])
        if sums:
            acc = out[-1]

    def after(x):
        nonlocal acc
        x, acc = lax.optimization_barrier((x, acc))
        return x

    near = exchanged(points, 2, 4)
    mate = swapped(points, 1)
    rows, own = call(row_kernel, (tile((2 * width, n), BF16), tile((n, width), BF16)), [points], name="rows")
    first(dict(own=own))
    cross = exchanged(after(points), 4, 2)
    first(dict(mate=mate))
    near = after(near)
    near_mate = swapped(near, 1)
    first(dict(near=near))
    diagonal = exchanged(after(near), 4, 2)
    cross_mate = swapped(cross, 1)
    first(dict(cross=cross, near_mate=near_mate))
    e, turned, sums = call(
        between_kernel,
        (tile((n, n)), tile((width, n), BF16), tile((3 * groups, 128))),
        [rows, near, cross, near_mate, cross_mate, done["near"][1], done["cross"][1], acc],
        scratch=[
            pltpu.VMEM((2 * width, n), BF16),
            pltpu.VMEM((n, 2 * width), BF16),
            pltpu.VMEM((n, 2 * width), BF16),
            pltpu.VMEM((n, width), BF16),
            pltpu.VMEM((n, 128), F32),
            pltpu.VMEM((8 * groups, 128), F32),
        ],
        name="between",
        tiles=2,
    )
    done["cross_mate"] = (e, turned)
    mate_sums = swapped(sums, 1)
    pack = call(pack_kernel, tile((6 * groups, 128)), [sums, mate_sums], name="pack")
    x, y, far = [swapped(pack, m) for m in (2, 4, 6)]
    packs = [far, x, y, pack]
    diagonal, pack = lax.optimization_barrier((diagonal, pack))
    diagonal_mate = swapped(diagonal, 1)
    first(dict(diagonal=diagonal), sums=False)
    first(dict(diagonal_mate=diagonal_mate), sums=False)
    masks = dict(
        own=(0, 0),
        mate=(1, 1),
        near=(2, 4),
        cross_mate=(3, 5),
        cross=(4, 2),
        near_mate=(5, 3),
        diagonal=(6, 6),
        diagonal_mate=(7, 7),
    )
    potential, displacement = call(
        functools.partial(second_kernel, total_points, list(masks.values())),
        (jax.ShapeDtypeStruct((groups, 128), F32), jax.ShapeDtypeStruct((n, width), F32)),
        [done[b][0] for b in masks] + [done[b][1] for b in masks] + packs + [own],
        scratch=[
            pltpu.VMEM((128, 128), F32),
            pltpu.VMEM((len(masks) * n, 128), F32),
            pltpu.VMEM((width, n), F32),
            pltpu.VMEM((8 * groups, 128), F32),
            pltpu.VMEM((groups, 128), F32),
            pltpu.VMEM((n, width), F32),
            pltpu.SemaphoreType.DMA((chunks + 1,)),
        ],
        out_specs=(IN_HBM, IN_HBM),
        name="second",
        tiles=len(masks),
    )
    return potential.reshape(n), displacement


def shifted(block, axis, distance):
    devices = range(lax.axis_size(axis))
    route = [((i - distance) % len(devices), i) for i in devices]
    return lax.ppermute(block, axis, route)


def square_norms(block_points):
    return jnp.sum(jnp.square(block_points.astype(jnp.float32)), axis=1)


def digit_set(offset, bit_index):
    return jnp.right_shift(offset, bit_index) % 2 == 1


def deliver_partner(block_points, offset):
    digits = lax.axis_size("rep").bit_length()
    current = block_points
    for bit_index in range(digits):
        arrived = shifted(current, "team", -(1 << bit_index))
        current = jnp.where(digit_set(offset, bit_index), arrived, current)
    return current


def deliver_mirror(block_points, offset):
    digits = lax.axis_size("rep").bit_length()
    current = block_points
    for bit_index in range(digits):
        arrived = shifted(current, "team", 1 << bit_index)
        current = jnp.where(digit_set(offset, bit_index), arrived, current)
    return current


def potential_partner(pot_one, offset):
    digits = lax.axis_size("rep").bit_length()
    current = pot_one
    for bit_index in range(digits):
        arrived = shifted(current, "team", -(1 << bit_index))
        current = jnp.where(digit_set(offset, bit_index), arrived, current)
    return current


def potential_mirror(pot_one, offset):
    digits = lax.axis_size("rep").bit_length()
    current = pot_one
    for bit_index in range(digits):
        arrived = shifted(current, "team", 1 << bit_index)
        current = jnp.where(digit_set(offset, bit_index), arrived, current)
    return current


def tile_sums(row_side, col_side, inv_eps, with_num):
    rows_x, rows_sq, rows_pot = row_side
    cols_x, cols_sq, cols_pot = col_side
    block_rows = rows_x.shape[0]
    numer_width = rows_x.shape[1] if with_num else 0
    col_count = 0
    row_block = min(block_rows, 512)
    col_block = min(block_rows, 256)
    cols_scale = jnp.exp(cols_pot * inv_eps)
    initial = (
        jnp.zeros((block_rows,), jnp.float32),
        jnp.zeros((block_rows, numer_width), jnp.float32),
        jnp.zeros((col_count,), jnp.float32),
        jnp.zeros((col_count, numer_width), jnp.float32),
    )

    def row_step(row_index, carried):
        row_total, row_numer, col_total, col_numer = carried
        row_start = row_index * row_block
        part_x = lax.dynamic_slice_in_dim(rows_x, row_start, row_block, 0)
        part_sq = lax.dynamic_slice_in_dim(rows_sq, row_start, row_block, 0)

        def col_step(col_index, inner_carried):
            block_total, block_numer, col_acc, col_num_acc = inner_carried
            col_start = col_index * col_block
            other_x = lax.dynamic_slice_in_dim(cols_x, col_start, col_block, 0)
            other_sq = lax.dynamic_slice_in_dim(cols_sq, col_start, col_block, 0)
            other_scale = lax.dynamic_slice_in_dim(cols_scale, col_start, col_block, 0)
            products = lax.dot_general(
                part_x, other_x, (((1,), (1,)), ((), ())), preferred_element_type=jnp.float32
            )
            kernel = jnp.exp(
                (products - 0.5 * part_sq[:, None] - 0.5 * other_sq[None, :]) * inv_eps
            )
            row_weight = kernel * other_scale[None, :]
            block_total = block_total + jnp.sum(row_weight, axis=1)
            if with_num:
                block_numer = block_numer + jnp.dot(
                    row_weight.astype(jnp.bfloat16), other_x, preferred_element_type=jnp.float32
                )
            return (block_total, block_numer, col_acc, col_num_acc)

        start_inner = (
            jnp.zeros((row_block,), jnp.float32),
            jnp.zeros((row_block, numer_width), jnp.float32),
            col_total,
            col_numer,
        )
        block_total, block_numer, col_total, col_numer = lax.fori_loop(
            0, block_rows // col_block, col_step, start_inner
        )
        row_total = lax.dynamic_update_slice_in_dim(row_total, block_total, row_start, 0)
        row_numer = lax.dynamic_update_slice_in_dim(row_numer, block_numer, row_start, 0)
        return (row_total, row_numer, col_total, col_numer)

    return lax.fori_loop(0, block_rows // row_block, row_step, initial)


def crossed_sums(own_side, partner_side, mirror_side, inv_eps, with_num):
    forward_part = tile_sums(own_side, partner_side, inv_eps, with_num)
    backward_part = tile_sums(own_side, mirror_side, inv_eps, with_num)
    return (forward_part[0] + backward_part[0], forward_part[1] + backward_part[1])


def neighbour_potentials(pot_one, offset, replica):
    partner_pot = potential_partner(pot_one, offset)
    mirror_pot = potential_mirror(pot_one, offset)
    mirror_pot = jnp.where(replica == 0, pot_one, mirror_pot)
    return (partner_pot, mirror_pot)


def looped_shards(points):
    block_rows = points.shape[0]
    replicas = lax.axis_size("rep")
    team_count = lax.axis_size("team")
    replica = lax.axis_index("rep")
    offset = jnp.where(replica == 0, replicas, replica)
    own_sq = square_norms(points)
    log_count = jnp.log(jnp.float32(block_rows * team_count))
    zero_pot = jnp.zeros((block_rows,), jnp.float32)
    partner_x = deliver_partner(points, offset)
    partner_sq = square_norms(partner_x)
    mirror_far = deliver_mirror(points, offset)
    mirror_x = jnp.where(replica == 0, points, mirror_far)
    mirror_sq = square_norms(mirror_x)
    first_local, unused_numer = crossed_sums(
        (points, own_sq, zero_pot),
        (partner_x, partner_sq, zero_pot),
        (mirror_x, mirror_sq, zero_pot),
        0.25,
        False,
    )
    first_sum = lax.psum(first_local, "rep")
    pot_one = 0.5 * (zero_pot - 4.0 * (jnp.log(first_sum) - log_count))
    partner_pot, mirror_pot = neighbour_potentials(pot_one, offset, replica)
    second_local, numer_local = crossed_sums(
        (points, own_sq, pot_one),
        (partner_x, partner_sq, partner_pot),
        (mirror_x, mirror_sq, mirror_pot),
        0.5,
        True,
    )
    second, numerator = lax.psum((second_local, numer_local), "rep")
    potential = 0.5 * (pot_one - 2.0 * (jnp.log(second) - log_count))
    displacement = points.astype(jnp.float32) - numerator / second[:, None]
    return (potential, displacement)


TILE_BYTES = 36 << 20


def solution(mesh):
    team = mesh.shape["team"]

    def body(points):
        n = points.shape[0]
        fits = 4 * n * n * team <= TILE_BYTES and team == 8 and n % 256 == 0
        return shards(points) if fits else looped_shards(points)

    return jax.shard_map(
        body,
        mesh=mesh,
        in_specs=(P("team", None),),
        out_specs=(P("team"), P("team", None)),
        check_vma=False,
    )
```

```python
import functools
import jax
import jax.numpy as jnp
from jax import lax
from jax.experimental import pallas as pl
from jax.experimental.pallas import tpu as pltpu
from jax.sharding import PartitionSpec as P

F32 = jnp.float32
BF16 = jnp.bfloat16
NT = (((1,), (1,)), ((), ()))
IN_VMEM = pl.BlockSpec(memory_space=pltpu.VMEM)
IN_HBM = pl.BlockSpec(memory_space=pl.ANY)
PARAMS = pltpu.CompilerParams(vmem_limit_bytes=16 << 20)


def kept(array):
    return pltpu.with_memory_space_constraint(array, pltpu.VMEM)


def swapped(array, mask):
    size = lax.axis_size("team")
    return lax.ppermute(array, "team", [(i, i ^ mask) for i in range(size)])


def exchanged(array, even, odd):
    size = lax.axis_size("team")
    return lax.ppermute(array, "team", [(i, i ^ (odd if i % 2 else even)) for i in range(size)])


def across(columns):
    row = lax.broadcasted_iota(jnp.int32, (128, 128), 0)
    diagonal = row == lax.broadcasted_iota(jnp.int32, (128, 128), 1)
    sums = [jnp.sum(columns[g : g + 128, :], axis=1, keepdims=True) for g in range(0, columns.shape[0], 128)]
    return [jnp.sum(jnp.where(diagonal, s, 0.0), axis=0, keepdims=True) for s in sums]


def pieces(x_turned):
    wide = x_turned.astype(F32)
    norms = jnp.sum(wide * wide, axis=0, keepdims=True)
    high = norms.astype(BF16).astype(F32)
    rest = norms - high
    middle = rest.astype(BF16).astype(F32)
    return high, middle, rest - middle


def put_columns(cols, part, x, x_turned):
    width = x.shape[1]
    high, middle, low = pieces(x_turned)
    sub = lax.broadcasted_iota(jnp.int32, (16, x.shape[0]), 0)
    extra = jnp.where(sub == 0, high, jnp.where(sub == 1, middle, jnp.where(sub == 2, low, 1.0))).astype(BF16)
    cols[part, :width] = x
    cols[part, width:] = jnp.concatenate([extra] * (width // 16), axis=0).T


def put_rows(rows, x_turned):
    width, n = x_turned.shape
    high, middle, low = pieces(x_turned)
    sub = lax.broadcasted_iota(jnp.int32, (16, n), 0)
    norm = jnp.where(sub == 3, high, jnp.where(sub == 4, middle, low))
    extra = jnp.where(sub < 3, -0.125, jnp.where(sub < 6, norm * -0.125, 0.0))
    rows[:width, :] = x_turned * jnp.asarray(0.25, BF16)
    rows[width : width + 16, :] = extra.astype(BF16)
    rows[width + 16 :, :] = jnp.zeros((width - 16, n), BF16)


def row_kernel(x_ref, rows_ref, own_ref):
    own_ref[...] = x_ref[...]
    put_rows(rows_ref, x_ref[...].T)


def put_tiles(rows_ref, x_refs, e_refs, turned_refs, col_refs, acc_in, acc_ref, along_ref):
    n = x_refs[0].shape[0]
    block = 256
    for i in range(0, n, block):
        groups = range(i // 128, (i + block) // 128)
        if acc_ref is not None:
            totals = [jnp.zeros((8, 128), F32) if acc_in is None else acc_in[8 * g : 8 * g + 8, :] for g in groups]
        for x_ref, e_ref, turned_ref, cols in zip(x_refs, e_refs, turned_refs, col_refs):
            for j in range(0, n, block):
                part = slice(j, j + block)
                if i == 0:
                    x_turned = x_ref[part, :].T
                    turned_ref[:, part] = x_turned
                    put_columns(cols, part, x_ref[part, :], x_turned)
                p = jnp.dot(cols[part, :], rows_ref[:, i : i + block], preferred_element_type=F32)
                sideways = along_ref is not None and x_ref is x_refs[-1]
                along = along_ref[part, :] if sideways and i else jnp.zeros((block, 128), F32)
                for t, g in enumerate(groups):
                    k = jnp.exp(p[:, t * 128 : (t + 1) * 128])
                    e_ref[part, g * 128 : g * 128 + 128] = k * k
                    if acc_ref is not None:
                        totals[t] = totals[t] + jnp.sum(k.reshape(block // 8, 8, 128), axis=0)
                    if sideways:
                        along = along + k
                if sideways:
                    along_ref[part, :] = along
        if acc_ref is not None:
            for t, g in enumerate(groups):
                acc_ref[8 * g : 8 * g + 8, :] = totals[t]


def first_kernel(count, start, sums, sideways, *refs):
    rows_ref, x_refs, refs = refs[0], refs[1 : 1 + count], refs[1 + count :]
    acc_in = acc_ref = along_ref = None
    if sums and not start:
        acc_in, refs = refs[0], refs[1:]
    e_refs, turned_refs, refs = refs[:count], refs[count : 2 * count], refs[2 * count :]
    if sums:
        acc_ref, refs = refs[0], refs[1:]
    if sideways:
        side_ref, along_ref, refs = refs[0], refs[-1], refs[1:-1]
    put_tiles(rows_ref, x_refs, e_refs, turned_refs, refs, acc_in, acc_ref, along_ref)
    if sideways:
        side_ref[...] = jnp.concatenate(across(along_ref[...]), axis=0)


def between_kernel(*refs):
    near_ref, cross_ref, near_mate_ref, cross_mate_ref, near_t, cross_t, acc_in, side_ref, *refs = refs
    out_ref, rows, cols, x, row_sums = refs
    me = lax.axis_index("team")
    core, side = me % 2, (me // 2) % 2
    n, width = near_ref.shape
    groups = n // 128
    block = 256

    @pl.when(core == 0)
    def _():
        rows[:width, :] = near_t[...]

    @pl.when(core == 1)
    def _():
        rows[:width, :] = cross_t[...]

    for which, (c, s) in ((cross_ref, (0, 0)), (near_ref, (1, 0)), (near_mate_ref, (0, 1)), (cross_mate_ref, (1, 1))):

        @pl.when((core == c) & (side == s))
        def _(which=which):
            x[...] = which[...]

    put_rows(rows, rows[:width, :])
    for j in range(0, n, block):
        part = slice(j, j + block)
        put_columns(cols, part, x[part, :], x[part, :].T)
        row_sums[part, :] = jnp.zeros((block, 128), F32)
    for i in range(0, n, block):
        totals = [jnp.zeros((8, 128), F32) for _ in range(block // 128)]
        for j in range(0, n, block):
            part = slice(j, j + block)
            p = jnp.dot(cols[part, :], rows[:, i : i + block], preferred_element_type=F32)
            along = row_sums[part, :]
            for t in range(block // 128):
                k = jnp.exp(p[:, t * 128 : (t + 1) * 128])
                along = along + k
                totals[t] = totals[t] + jnp.sum(k.reshape(block // 8, 8, 128), axis=0)
            row_sums[part, :] = along
        for t, total in enumerate(totals):
            g = groups + i // 128 + t
            out_ref[g : g + 1, :] = jnp.sum(total, axis=0, keepdims=True)
    out_ref[2 * groups : 3 * groups, :] = jnp.concatenate(across(row_sums[...]), axis=0)
    out_ref[3 * groups :, :] = side_ref[...]
    for g in range(groups):
        out_ref[g : g + 1, :] = jnp.sum(acc_in[8 * g : 8 * g + 8, :], axis=0, keepdims=True)


def pack_kernel(*refs):
    step = refs[0].shape[0]
    for t, ref in enumerate(refs[:-1]):
        refs[-1][t * step : (t + 1) * step, :] = ref[...]


PARTS = (((0,), (1, 2)), ((1, 2), (3, 4, 5)), ((3, 4, 5), (6, 7)), ((6, 7), ()))


def second_kernel(points, masks, *refs):
    count = len(masks)
    e_refs, refs = refs[:count], refs[count:]
    x_refs, refs = refs[:count], refs[count:]
    pack_refs, refs = refs[:5], refs[5:]
    own_ref, pot_hbm, out_hbm, shares_ref, scales, num_ref, acc_ref, pot_ref, out_ref, sems = refs
    width, n = x_refs[0].shape
    groups = n // 128
    block = 256
    team = lax.axis_index("team")
    core, side = team % 2, team // 2 % 2

    def message(mask, slot):
        if mask >= 6:
            return pack_refs[mask - 6][slot * groups : (slot + 1) * groups, :]
        first = (mask % 2 * 4 + slot) * groups
        return pack_refs[(4, 2, 3)[mask // 2]][first : first + groups, :]

    def first_sum(mask):
        near = message(mask, 0) + message(mask ^ 2, 1)
        near = near + jnp.where(side == mask // 2 % 2, message(mask ^ 4, 2), message(mask ^ 5, 2))
        return near + jnp.where(core == mask % 2, message(mask ^ 3, 3), message(mask ^ 5, 3))

    sums = [first_sum(mask) for mask in range(count)]
    order = [sums[even] if even == odd else jnp.where(core == 0, sums[even], sums[odd]) for even, odd in masks]
    shares = float(points) / jnp.concatenate(order, axis=0)
    shares_ref[...] = jnp.concatenate([shares, jnp.zeros((128 - count * groups, 128), F32)], axis=0).T

    def put_scales(t):
        for g in range(groups):
            first = t * n + g * 128
            lane = t * groups + g
            scales[first : first + 128, :] = jnp.broadcast_to(shares_ref[:, lane : lane + 1], (128, 128))

    def part(tiles, ahead):
        start = tiles[0] == 0
        for t in ahead:
            put_scales(t)
        for i in range(0, n, block):
            cols = slice(i, i + block)
            lanes = range(i, i + block, 128)
            numerator = jnp.zeros((width, block), F32) if start else num_ref[:, cols]
            totals = [jnp.zeros((8, 128), F32) if start else acc_ref[l // 16 : l // 16 + 8, :] for l in lanes]
            for t in tiles:
                for j in range(0, n, block):
                    scale = scales[t * n + j : t * n + j + block, :]
                    weights = []
                    for u, l in enumerate(lanes):
                        w = e_refs[t][j : j + block, l : l + 128] * scale
                        totals[u] = totals[u] + jnp.sum(w.reshape(block // 8, 8, 128), axis=0)
                        weights.append(w.astype(BF16))
                    weight = jnp.concatenate(weights, axis=1)
                    numerator = numerator + jnp.dot(x_refs[t][:, j : j + block], weight, preferred_element_type=F32)
            for u, l in enumerate(lanes):
                acc_ref[l // 16 : l // 16 + 8, :] = totals[u]
            num_ref[:, cols] = numerator

    def out_copy(i):
        rows = slice(i * block, (i + 1) * block)
        return pltpu.make_async_copy(out_ref.at[rows, :], out_hbm.at[rows, :], sems.at[i])

    put_scales(0)
    for tiles, ahead in PARTS:
        pl.when(team >= 0)(functools.partial(part, tiles, ahead))
    seconds = []
    for g in range(groups):
        rows = slice(g * 128, (g + 1) * 128)
        seconds.append(jnp.sum(acc_ref[8 * g : 8 * g + 8, :], axis=0, keepdims=True))
        out_ref[rows, :] = own_ref[rows, :].astype(F32) - (num_ref[:, rows] / seconds[-1]).T
        if (g + 1) * 128 % block == 0:
            out_copy(g * 128 // block).start()
    log_count = jnp.log(jnp.float32(points))
    second = jnp.concatenate(seconds, axis=0)
    pot_one = -2.0 * (jnp.log(sums[0]) - log_count)
    pot_ref[...] = 0.5 * (pot_one - 2.0 * (jnp.log(second) - log_count))
    pot_copy = pltpu.make_async_copy(pot_ref, pot_hbm, sems.at[n // block])
    pot_copy.start()
    for i in range(n // block):
        out_copy(i).wait()
    pot_copy.wait()


def shards(points):
    n, width = points.shape
    total_points = n * lax.axis_size("team")
    groups = n // 128
    chunks = n // 256

    def tile(shape, dtype=F32):
        return pltpu.VMEM(shape, dtype)

    def call(kernel, out_shape, args, scratch=(), out_specs=None, name=None, tiles=0):
        single = not isinstance(out_shape, tuple)
        specs = out_specs or (IN_VMEM if single else tuple(IN_VMEM for _ in out_shape))
        return pl.pallas_call(
            kernel,
            out_shape=out_shape,
            in_specs=[IN_VMEM] * len(args),
            out_specs=specs,
            scratch_shapes=list(scratch),
            compiler_params=PARAMS,
            cost_estimate=pl.CostEstimate(flops=tiles * 24 * n * n * width, bytes_accessed=0, transcendentals=0),
            name=name,
        )(*[kept(a) for a in args])

    acc = None
    done = {}

    def first(blocks, sums=True, sideways=False):
        nonlocal acc
        count = len(blocks)
        out = call(
            functools.partial(first_kernel, count, acc is None, sums, sideways),
            (tile((n, n)),) * count
            + (tile((width, n), BF16),) * count
            + (tile((8 * groups, 128)),) * sums
            + (tile((groups, 128)),) * sideways,
            [rows, *blocks.values()] + ([acc] if sums and acc is not None else []),
            scratch=[pltpu.VMEM((n, 2 * width), BF16)] * count + [pltpu.VMEM((n, 128), F32)] * sideways,
            name="first",
            tiles=count,
        )
        for t, block in enumerate(blocks):
            done[block] = (out[t], out[count + t])
        if sums:
            acc = out[2 * count]
        return out[-1]

    def after(x):
        nonlocal acc
        x, acc = lax.optimization_barrier((x, acc))
        return x

    near = exchanged(points, 2, 4)
    mate = swapped(points, 1)
    rows, own = call(row_kernel, (tile((2 * width, n), BF16), tile((n, width), BF16)), [points], name="rows")
    first(dict(own=own))
    cross = exchanged(after(points), 4, 2)
    first(dict(mate=mate))
    near = after(near)
    near_mate = swapped(near, 1)
    first(dict(near=near))
    diagonal = exchanged(after(near), 4, 2)
    cross_mate = swapped(cross, 1)
    side = first(dict(cross=cross, near_mate=near_mate), sideways=True)
    sums = call(
        between_kernel,
        tile((4 * groups, 128)),
        [near, cross, near_mate, cross_mate, done["near"][1], done["cross"][1], acc, side],
        scratch=[
            pltpu.VMEM((2 * width, n), BF16),
            pltpu.VMEM((n, 2 * width), BF16),
            pltpu.VMEM((n, width), BF16),
            pltpu.VMEM((n, 128), F32),
        ],
        name="between",
        tiles=1,
    )
    far = swapped(sums, 6)
    mate_sums = swapped(sums, 1)
    pack = call(pack_kernel, tile((8 * groups, 128)), [sums, mate_sums], name="pack")
    x, y = [swapped(pack, m) for m in (2, 4)]
    cross_mate, diagonal, pack = lax.optimization_barrier((cross_mate, diagonal, pack))
    diagonal_mate = swapped(diagonal, 1)
    first(dict(cross_mate=cross_mate, diagonal=diagonal), sums=False)
    e, far = lax.optimization_barrier((done["diagonal"][0], far))
    done["diagonal"] = (e, done["diagonal"][1])
    far_mate = swapped(far, 1)
    first(dict(diagonal_mate=diagonal_mate), sums=False)
    packs = [far, far_mate, x, y, pack]
    masks = dict(
        own=(0, 0),
        mate=(1, 1),
        near=(2, 4),
        cross_mate=(3, 5),
        cross=(4, 2),
        near_mate=(5, 3),
        diagonal=(6, 6),
        diagonal_mate=(7, 7),
    )
    potential, displacement = call(
        functools.partial(second_kernel, total_points, list(masks.values())),
        (jax.ShapeDtypeStruct((groups, 128), F32), jax.ShapeDtypeStruct((n, width), F32)),
        [done[b][0] for b in masks] + [done[b][1] for b in masks] + packs + [own],
        scratch=[
            pltpu.VMEM((128, 128), F32),
            pltpu.VMEM((len(masks) * n, 128), F32),
            pltpu.VMEM((width, n), F32),
            pltpu.VMEM((8 * groups, 128), F32),
            pltpu.VMEM((groups, 128), F32),
            pltpu.VMEM((n, width), F32),
            pltpu.SemaphoreType.DMA((chunks + 1,)),
        ],
        out_specs=(IN_HBM, IN_HBM),
        name="second",
        tiles=len(masks),
    )
    return potential.reshape(n), displacement


def shifted(block, axis, distance):
    devices = range(lax.axis_size(axis))
    route = [((i - distance) % len(devices), i) for i in devices]
    return lax.ppermute(block, axis, route)


def square_norms(block_points):
    return jnp.sum(jnp.square(block_points.astype(jnp.float32)), axis=1)


def digit_set(offset, bit_index):
    return jnp.right_shift(offset, bit_index) % 2 == 1


def deliver_partner(block_points, offset):
    digits = lax.axis_size("rep").bit_length()
    current = block_points
    for bit_index in range(digits):
        arrived = shifted(current, "team", -(1 << bit_index))
        current = jnp.where(digit_set(offset, bit_index), arrived, current)
    return current


def deliver_mirror(block_points, offset):
    digits = lax.axis_size("rep").bit_length()
    current = block_points
    for bit_index in range(digits):
        arrived = shifted(current, "team", 1 << bit_index)
        current = jnp.where(digit_set(offset, bit_index), arrived, current)
    return current


def potential_partner(pot_one, offset):
    digits = lax.axis_size("rep").bit_length()
    current = pot_one
    for bit_index in range(digits):
        arrived = shifted(current, "team", -(1 << bit_index))
        current = jnp.where(digit_set(offset, bit_index), arrived, current)
    return current


def potential_mirror(pot_one, offset):
    digits = lax.axis_size("rep").bit_length()
    current = pot_one
    for bit_index in range(digits):
        arrived = shifted(current, "team", 1 << bit_index)
        current = jnp.where(digit_set(offset, bit_index), arrived, current)
    return current


def tile_sums(row_side, col_side, inv_eps, with_num):
    rows_x, rows_sq, rows_pot = row_side
    cols_x, cols_sq, cols_pot = col_side
    block_rows = rows_x.shape[0]
    numer_width = rows_x.shape[1] if with_num else 0
    col_count = 0
    row_block = min(block_rows, 512)
    col_block = min(block_rows, 256)
    cols_scale = jnp.exp(cols_pot * inv_eps)
    initial = (
        jnp.zeros((block_rows,), jnp.float32),
        jnp.zeros((block_rows, numer_width), jnp.float32),
        jnp.zeros((col_count,), jnp.float32),
        jnp.zeros((col_count, numer_width), jnp.float32),
    )

    def row_step(row_index, carried):
        row_total, row_numer, col_total, col_numer = carried
        row_start = row_index * row_block
        part_x = lax.dynamic_slice_in_dim(rows_x, row_start, row_block, 0)
        part_sq = lax.dynamic_slice_in_dim(rows_sq, row_start, row_block, 0)

        def col_step(col_index, inner_carried):
            block_total, block_numer, col_acc, col_num_acc = inner_carried
            col_start = col_index * col_block
            other_x = lax.dynamic_slice_in_dim(cols_x, col_start, col_block, 0)
            other_sq = lax.dynamic_slice_in_dim(cols_sq, col_start, col_block, 0)
            other_scale = lax.dynamic_slice_in_dim(cols_scale, col_start, col_block, 0)
            products = lax.dot_general(
                part_x, other_x, (((1,), (1,)), ((), ())), preferred_element_type=jnp.float32
            )
            kernel = jnp.exp(
                (products - 0.5 * part_sq[:, None] - 0.5 * other_sq[None, :]) * inv_eps
            )
            row_weight = kernel * other_scale[None, :]
            block_total = block_total + jnp.sum(row_weight, axis=1)
            if with_num:
                block_numer = block_numer + jnp.dot(
                    row_weight.astype(jnp.bfloat16), other_x, preferred_element_type=jnp.float32
                )
            return (block_total, block_numer, col_acc, col_num_acc)

        start_inner = (
            jnp.zeros((row_block,), jnp.float32),
            jnp.zeros((row_block, numer_width), jnp.float32),
            col_total,
            col_numer,
        )
        block_total, block_numer, col_total, col_numer = lax.fori_loop(
            0, block_rows // col_block, col_step, start_inner
        )
        row_total = lax.dynamic_update_slice_in_dim(row_total, block_total, row_start, 0)
        row_numer = lax.dynamic_update_slice_in_dim(row_numer, block_numer, row_start, 0)
        return (row_total, row_numer, col_total, col_numer)

    return lax.fori_loop(0, block_rows // row_block, row_step, initial)


def crossed_sums(own_side, partner_side, mirror_side, inv_eps, with_num):
    forward_part = tile_sums(own_side, partner_side, inv_eps, with_num)
    backward_part = tile_sums(own_side, mirror_side, inv_eps, with_num)
    return (forward_part[0] + backward_part[0], forward_part[1] + backward_part[1])


def neighbour_potentials(pot_one, offset, replica):
    partner_pot = potential_partner(pot_one, offset)
    mirror_pot = potential_mirror(pot_one, offset)
    mirror_pot = jnp.where(replica == 0, pot_one, mirror_pot)
    return (partner_pot, mirror_pot)


def looped_shards(points):
    block_rows = points.shape[0]
    replicas = lax.axis_size("rep")
    team_count = lax.axis_size("team")
    replica = lax.axis_index("rep")
    offset = jnp.where(replica == 0, replicas, replica)
    own_sq = square_norms(points)
    log_count = jnp.log(jnp.float32(block_rows * team_count))
    zero_pot = jnp.zeros((block_rows,), jnp.float32)
    partner_x = deliver_partner(points, offset)
    partner_sq = square_norms(partner_x)
    mirror_far = deliver_mirror(points, offset)
    mirror_x = jnp.where(replica == 0, points, mirror_far)
    mirror_sq = square_norms(mirror_x)
    first_local, unused_numer = crossed_sums(
        (points, own_sq, zero_pot),
        (partner_x, partner_sq, zero_pot),
        (mirror_x, mirror_sq, zero_pot),
        0.25,
        False,
    )
    first_sum = lax.psum(first_local, "rep")
    pot_one = 0.5 * (zero_pot - 4.0 * (jnp.log(first_sum) - log_count))
    partner_pot, mirror_pot = neighbour_potentials(pot_one, offset, replica)
    second_local, numer_local = crossed_sums(
        (points, own_sq, pot_one),
        (partner_x, partner_sq, partner_pot),
        (mirror_x, mirror_sq, mirror_pot),
        0.5,
        True,
    )
    second, numerator = lax.psum((second_local, numer_local), "rep")
    potential = 0.5 * (pot_one - 2.0 * (jnp.log(second) - log_count))
    displacement = points.astype(jnp.float32) - numerator / second[:, None]
    return (potential, displacement)


TILE_BYTES = 36 << 20


def solution(mesh):
    team = mesh.shape["team"]

    def body(points):
        n = points.shape[0]
        fits = 4 * n * n * team <= TILE_BYTES and team == 8 and n % 256 == 0
        return shards(points) if fits else looped_shards(points)

    return jax.shard_map(
        body,
        mesh=mesh,
        in_specs=(P("team", None),),
        out_specs=(P("team"), P("team", None)),
        check_vma=False,
    )
```

```python
import functools
import jax
import jax.numpy as jnp
from jax import lax
from jax.experimental import pallas as pl
from jax.experimental.pallas import tpu as pltpu
from jax.sharding import PartitionSpec as P

F32 = jnp.float32
BF16 = jnp.bfloat16
NT = (((1,), (1,)), ((), ()))
IN_VMEM = pl.BlockSpec(memory_space=pltpu.VMEM)
IN_HBM = pl.BlockSpec(memory_space=pl.ANY)
PARAMS = pltpu.CompilerParams(vmem_limit_bytes=16 << 20)


def kept(array):
    return pltpu.with_memory_space_constraint(array, pltpu.VMEM)


def swapped(array, mask):
    size = lax.axis_size("team")
    return lax.ppermute(array, "team", [(i, i ^ mask) for i in range(size)])


def exchanged(array, even, odd):
    size = lax.axis_size("team")
    return lax.ppermute(array, "team", [(i, i ^ (odd if i % 2 else even)) for i in range(size)])


def across(columns):
    row = lax.broadcasted_iota(jnp.int32, (128, 128), 0)
    diagonal = row == lax.broadcasted_iota(jnp.int32, (128, 128), 1)
    sums = [jnp.sum(columns[g : g + 128, :], axis=1, keepdims=True) for g in range(0, columns.shape[0], 128)]
    return [jnp.sum(jnp.where(diagonal, s, 0.0), axis=0, keepdims=True) for s in sums]


def pieces(x_turned):
    wide = x_turned.astype(F32)
    norms = jnp.sum(wide * wide, axis=0, keepdims=True)
    high = norms.astype(BF16).astype(F32)
    rest = norms - high
    middle = rest.astype(BF16).astype(F32)
    return high, middle, rest - middle


def put_columns(cols, part, x, x_turned):
    width = x.shape[1]
    high, middle, low = pieces(x_turned)
    sub = lax.broadcasted_iota(jnp.int32, (16, x.shape[0]), 0)
    extra = jnp.where(sub == 0, high, jnp.where(sub == 1, middle, jnp.where(sub == 2, low, 1.0))).astype(BF16)
    cols[part, :width] = x
    cols[part, width:] = jnp.concatenate([extra] * (width // 16), axis=0).T


def put_rows(rows, x_turned):
    width, n = x_turned.shape
    high, middle, low = pieces(x_turned)
    sub = lax.broadcasted_iota(jnp.int32, (16, n), 0)
    norm = jnp.where(sub == 3, high, jnp.where(sub == 4, middle, low))
    extra = jnp.where(sub < 3, -0.125, jnp.where(sub < 6, norm * -0.125, 0.0))
    rows[:width, :] = x_turned * jnp.asarray(0.25, BF16)
    rows[width : width + 16, :] = extra.astype(BF16)
    rows[width + 16 :, :] = jnp.zeros((width - 16, n), BF16)


def row_kernel(x_ref, rows_ref, own_ref):
    own_ref[...] = x_ref[...]
    put_rows(rows_ref, x_ref[...].T)


def put_tiles(rows_ref, x_refs, e_refs, turned_refs, col_refs, acc_in, acc_ref, along_ref):
    n = x_refs[0].shape[0]
    block = 256
    for i in range(0, n, block):
        groups = range(i // 128, (i + block) // 128)
        if acc_ref is not None:
            totals = [jnp.zeros((8, 128), F32) if acc_in is None else acc_in[8 * g : 8 * g + 8, :] for g in groups]
        for x_ref, e_ref, turned_ref, cols in zip(x_refs, e_refs, turned_refs, col_refs):
            for j in range(0, n, block):
                part = slice(j, j + block)
                if i == 0:
                    x_turned = x_ref[part, :].T
                    turned_ref[:, part] = x_turned
                    put_columns(cols, part, x_ref[part, :], x_turned)
                p = jnp.dot(cols[part, :], rows_ref[:, i : i + block], preferred_element_type=F32)
                sideways = along_ref is not None and x_ref is x_refs[-1]
                along = along_ref[part, :] if sideways and i else jnp.zeros((block, 128), F32)
                for t, g in enumerate(groups):
                    k = jnp.exp(p[:, t * 128 : (t + 1) * 128])
                    e_ref[part, g * 128 : g * 128 + 128] = k * k
                    if acc_ref is not None:
                        totals[t] = totals[t] + jnp.sum(k.reshape(block // 8, 8, 128), axis=0)
                    if sideways:
                        along = along + k
                if sideways:
                    along_ref[part, :] = along
        if acc_ref is not None:
            for t, g in enumerate(groups):
                acc_ref[8 * g : 8 * g + 8, :] = totals[t]


def first_kernel(count, start, sums, as_rows, *refs):
    rows_ref, x_refs, refs = refs[0], refs[1 : 1 + count], refs[1 + count :]
    acc_in = acc_ref = None
    if sums and not start:
        acc_in, refs = refs[0], refs[1:]
    e_refs, turned_refs, refs = refs[:count], refs[count : 2 * count], refs[2 * count :]
    if sums:
        acc_ref, refs = refs[0], refs[1:]
    if as_rows:
        put_rows(refs[0], x_refs[0][...].T)
        refs = refs[1:]
    put_tiles(rows_ref, x_refs, e_refs, turned_refs, refs, acc_in, acc_ref, None)


def third_kernel(*refs):
    rows_ref, near_rows, cross_ref, near_mate_ref, acc_in, *refs = refs
    e_cross, e_mate, cross_t, mate_t, out_ref, cross_cols, mate_cols, along, between, acc = refs
    team = lax.axis_index("team")
    with_mate = team % 2 == team // 2 % 2
    n = cross_ref.shape[0]
    groups = n // 128
    block = 256
    put_tiles(
        rows_ref,
        [cross_ref, near_mate_ref],
        [e_cross, e_mate],
        [cross_t, mate_t],
        [cross_cols, mate_cols],
        acc_in,
        acc,
        along,
    )
    for i in range(0, n, block):
        totals = [jnp.zeros((8, 128), F32) for _ in range(block // 128)]
        for j in range(0, n, block):
            part = slice(j, j + block)
            cols = jnp.where(with_mate, mate_cols[part, :], cross_cols[part, :])
            p = jnp.dot(cols, near_rows[:, i : i + block], preferred_element_type=F32)
            over = between[part, :] if i else jnp.zeros((block, 128), F32)
            for t in range(block // 128):
                k = jnp.exp(p[:, t * 128 : (t + 1) * 128])
                over = over + k
                totals[t] = totals[t] + jnp.sum(k.reshape(block // 8, 8, 128), axis=0)
            between[part, :] = over
        for t, total in enumerate(totals):
            g = groups + i // 128 + t
            out_ref[g : g + 1, :] = jnp.sum(total, axis=0, keepdims=True)
    out_ref[2 * groups : 3 * groups, :] = jnp.concatenate(across(between[...]), axis=0)
    out_ref[3 * groups :, :] = jnp.concatenate(across(along[...]), axis=0)
    for g in range(groups):
        out_ref[g : g + 1, :] = jnp.sum(acc[8 * g : 8 * g + 8, :], axis=0, keepdims=True)


def pack_kernel(*refs):
    step = refs[0].shape[0]
    for t, ref in enumerate(refs[:-1]):
        refs[-1][t * step : (t + 1) * step, :] = ref[...]


PARTS = (((0,), (1, 2)), ((1, 2), (3, 4, 5)), ((3, 4, 5), (6, 7)), ((6, 7), ()))


def second_kernel(points, masks, *refs):
    count = len(masks)
    e_refs, refs = refs[:count], refs[count:]
    x_refs, refs = refs[:count], refs[count:]
    pack_refs, refs = refs[:5], refs[5:]
    own_ref, pot_hbm, out_hbm, shares_ref, scales, num_ref, acc_ref, pot_ref, out_ref, sems = refs
    width, n = x_refs[0].shape
    groups = n // 128
    block = 256
    team = lax.axis_index("team")
    core, side = team % 2, team // 2 % 2

    def message(mask, slot):
        if mask >= 6:
            return pack_refs[mask - 6][slot * groups : (slot + 1) * groups, :]
        first = (mask % 2 * 4 + slot) * groups
        return pack_refs[(4, 2, 3)[mask // 2]][first : first + groups, :]

    def first_sum(mask):
        even, low = core == mask % 2, side == mask // 2 % 2
        two, three, four, five = mask ^ 2, mask ^ 3, mask ^ 4, mask ^ 5
        total = message(mask, 0) + jnp.where(even, message(two, 1), message(four, 1))
        at_low = jnp.where(even, message(three, 2), message(five, 2))
        at_high = jnp.where(even, message(four, 2), message(two, 2))
        return total + jnp.where(low, at_low, at_high) + jnp.where(even, message(three, 3), message(five, 3))

    sums = [first_sum(mask) for mask in range(count)]
    order = [sums[even] if even == odd else jnp.where(core == 0, sums[even], sums[odd]) for even, odd in masks]
    shares = float(points) / jnp.concatenate(order, axis=0)
    shares_ref[...] = jnp.concatenate([shares, jnp.zeros((128 - count * groups, 128), F32)], axis=0).T

    def put_scales(t):
        for g in range(groups):
            first = t * n + g * 128
            lane = t * groups + g
            scales[first : first + 128, :] = jnp.broadcast_to(shares_ref[:, lane : lane + 1], (128, 128))

    def part(tiles, ahead):
        start = tiles[0] == 0
        for t in ahead:
            put_scales(t)
        for i in range(0, n, block):
            cols = slice(i, i + block)
            lanes = range(i, i + block, 128)
            numerator = jnp.zeros((width, block), F32) if start else num_ref[:, cols]
            totals = [jnp.zeros((8, 128), F32) if start else acc_ref[l // 16 : l // 16 + 8, :] for l in lanes]
            for t in tiles:
                for j in range(0, n, block):
                    scale = scales[t * n + j : t * n + j + block, :]
                    weights = []
                    for u, l in enumerate(lanes):
                        w = e_refs[t][j : j + block, l : l + 128] * scale
                        totals[u] = totals[u] + jnp.sum(w.reshape(block // 8, 8, 128), axis=0)
                        weights.append(w.astype(BF16))
                    weight = jnp.concatenate(weights, axis=1)
                    numerator = numerator + jnp.dot(x_refs[t][:, j : j + block], weight, preferred_element_type=F32)
            for u, l in enumerate(lanes):
                acc_ref[l // 16 : l // 16 + 8, :] = totals[u]
            num_ref[:, cols] = numerator

    def out_copy(i):
        rows = slice(i * block, (i + 1) * block)
        return pltpu.make_async_copy(out_ref.at[rows, :], out_hbm.at[rows, :], sems.at[i])

    put_scales(0)
    for tiles, ahead in PARTS:
        pl.when(team >= 0)(functools.partial(part, tiles, ahead))
    seconds = []
    for g in range(groups):
        rows = slice(g * 128, (g + 1) * 128)
        seconds.append(jnp.sum(acc_ref[8 * g : 8 * g + 8, :], axis=0, keepdims=True))
        out_ref[rows, :] = own_ref[rows, :].astype(F32) - (num_ref[:, rows] / seconds[-1]).T
        if (g + 1) * 128 % block == 0:
            out_copy(g * 128 // block).start()
    log_count = jnp.log(jnp.float32(points))
    second = jnp.concatenate(seconds, axis=0)
    pot_one = -2.0 * (jnp.log(sums[0]) - log_count)
    pot_ref[...] = 0.5 * (pot_one - 2.0 * (jnp.log(second) - log_count))
    pot_copy = pltpu.make_async_copy(pot_ref, pot_hbm, sems.at[n // block])
    pot_copy.start()
    for i in range(n // block):
        out_copy(i).wait()
    pot_copy.wait()


def shards(points):
    n, width = points.shape
    total_points = n * lax.axis_size("team")
    groups = n // 128
    chunks = n // 256

    def tile(shape, dtype=F32):
        return pltpu.VMEM(shape, dtype)

    def call(kernel, out_shape, args, scratch=(), out_specs=None, name=None, tiles=0):
        single = not isinstance(out_shape, tuple)
        specs = out_specs or (IN_VMEM if single else tuple(IN_VMEM for _ in out_shape))
        return pl.pallas_call(
            kernel,
            out_shape=out_shape,
            in_specs=[IN_VMEM] * len(args),
            out_specs=specs,
            scratch_shapes=list(scratch),
            compiler_params=PARAMS,
            cost_estimate=pl.CostEstimate(flops=tiles * 24 * n * n * width, bytes_accessed=0, transcendentals=0),
            name=name,
        )(*[kept(a) for a in args])

    acc = None
    done = {}

    def first(blocks, sums=True, as_rows=False):
        nonlocal acc
        count = len(blocks)
        out = call(
            functools.partial(first_kernel, count, acc is None, sums, as_rows),
            (tile((n, n)),) * count
            + (tile((width, n), BF16),) * count
            + (tile((8 * groups, 128)),) * sums
            + (tile((2 * width, n), BF16),) * as_rows,
            [rows, *blocks.values()] + ([acc] if sums and acc is not None else []),
            scratch=[pltpu.VMEM((n, 2 * width), BF16)] * count,
            name="first",
            tiles=count,
        )
        for t, block in enumerate(blocks):
            done[block] = (out[t], out[count + t])
        if sums:
            acc = out[2 * count]
        return out[-1]

    def after(x):
        nonlocal acc
        x, acc = lax.optimization_barrier((x, acc))
        return x

    near = exchanged(points, 2, 4)
    mate = swapped(points, 1)
    rows, own = call(row_kernel, (tile((2 * width, n), BF16), tile((n, width), BF16)), [points], name="rows")
    first(dict(own=own))
    cross = exchanged(after(points), 4, 2)
    first(dict(mate=mate))
    near = after(near)
    near_mate = swapped(near, 1)
    near_rows = first(dict(near=near), as_rows=True)
    diagonal = exchanged(after(near), 4, 2)
    cross_mate = swapped(cross, 1)
    *out, sums = call(
        third_kernel,
        (tile((n, n)),) * 2 + (tile((width, n), BF16),) * 2 + (tile((4 * groups, 128)),),
        [rows, near_rows, cross, near_mate, acc],
        scratch=[
            pltpu.VMEM((n, 2 * width), BF16),
            pltpu.VMEM((n, 2 * width), BF16),
            pltpu.VMEM((n, 128), F32),
            pltpu.VMEM((n, 128), F32),
            pltpu.VMEM((8 * groups, 128), F32),
        ],
        name="between",
        tiles=3,
    )
    done["cross"], done["near_mate"] = (out[0], out[2]), (out[1], out[3])
    far = swapped(sums, 6)
    mate_sums = swapped(sums, 1)
    pack = call(pack_kernel, tile((8 * groups, 128)), [sums, mate_sums], name="pack")
    x, y = [swapped(pack, m) for m in (2, 4)]
    cross_mate, diagonal, pack = lax.optimization_barrier((cross_mate, diagonal, pack))
    diagonal_mate = swapped(diagonal, 1)
    first(dict(cross_mate=cross_mate, diagonal=diagonal), sums=False)
    e, far = lax.optimization_barrier((done["diagonal"][0], far))
    done["diagonal"] = (e, done["diagonal"][1])
    far_mate = swapped(far, 1)
    first(dict(diagonal_mate=diagonal_mate), sums=False)
    packs = [far, far_mate, x, y, pack]
    masks = dict(
        own=(0, 0),
        mate=(1, 1),
        near=(2, 4),
        cross_mate=(3, 5),
        cross=(4, 2),
        near_mate=(5, 3),
        diagonal=(6, 6),
        diagonal_mate=(7, 7),
    )
    potential, displacement = call(
        functools.partial(second_kernel, total_points, list(masks.values())),
        (jax.ShapeDtypeStruct((groups, 128), F32), jax.ShapeDtypeStruct((n, width), F32)),
        [done[b][0] for b in masks] + [done[b][1] for b in masks] + packs + [own],
        scratch=[
            pltpu.VMEM((128, 128), F32),
            pltpu.VMEM((len(masks) * n, 128), F32),
            pltpu.VMEM((width, n), F32),
            pltpu.VMEM((8 * groups, 128), F32),
            pltpu.VMEM((groups, 128), F32),
            pltpu.VMEM((n, width), F32),
            pltpu.SemaphoreType.DMA((chunks + 1,)),
        ],
        out_specs=(IN_HBM, IN_HBM),
        name="second",
        tiles=len(masks),
    )
    return potential.reshape(n), displacement


def shifted(block, axis, distance):
    devices = range(lax.axis_size(axis))
    route = [((i - distance) % len(devices), i) for i in devices]
    return lax.ppermute(block, axis, route)


def square_norms(block_points):
    return jnp.sum(jnp.square(block_points.astype(jnp.float32)), axis=1)


def digit_set(offset, bit_index):
    return jnp.right_shift(offset, bit_index) % 2 == 1


def deliver_partner(block_points, offset):
    digits = lax.axis_size("rep").bit_length()
    current = block_points
    for bit_index in range(digits):
        arrived = shifted(current, "team", -(1 << bit_index))
        current = jnp.where(digit_set(offset, bit_index), arrived, current)
    return current


def deliver_mirror(block_points, offset):
    digits = lax.axis_size("rep").bit_length()
    current = block_points
    for bit_index in range(digits):
        arrived = shifted(current, "team", 1 << bit_index)
        current = jnp.where(digit_set(offset, bit_index), arrived, current)
    return current


def potential_partner(pot_one, offset):
    digits = lax.axis_size("rep").bit_length()
    current = pot_one
    for bit_index in range(digits):
        arrived = shifted(current, "team", -(1 << bit_index))
        current = jnp.where(digit_set(offset, bit_index), arrived, current)
    return current


def potential_mirror(pot_one, offset):
    digits = lax.axis_size("rep").bit_length()
    current = pot_one
    for bit_index in range(digits):
        arrived = shifted(current, "team", 1 << bit_index)
        current = jnp.where(digit_set(offset, bit_index), arrived, current)
    return current


def tile_sums(row_side, col_side, inv_eps, with_num):
    rows_x, rows_sq, rows_pot = row_side
    cols_x, cols_sq, cols_pot = col_side
    block_rows = rows_x.shape[0]
    numer_width = rows_x.shape[1] if with_num else 0
    col_count = 0
    row_block = min(block_rows, 512)
    col_block = min(block_rows, 256)
    cols_scale = jnp.exp(cols_pot * inv_eps)
    initial = (
        jnp.zeros((block_rows,), jnp.float32),
        jnp.zeros((block_rows, numer_width), jnp.float32),
        jnp.zeros((col_count,), jnp.float32),
        jnp.zeros((col_count, numer_width), jnp.float32),
    )

    def row_step(row_index, carried):
        row_total, row_numer, col_total, col_numer = carried
        row_start = row_index * row_block
        part_x = lax.dynamic_slice_in_dim(rows_x, row_start, row_block, 0)
        part_sq = lax.dynamic_slice_in_dim(rows_sq, row_start, row_block, 0)

        def col_step(col_index, inner_carried):
            block_total, block_numer, col_acc, col_num_acc = inner_carried
            col_start = col_index * col_block
            other_x = lax.dynamic_slice_in_dim(cols_x, col_start, col_block, 0)
            other_sq = lax.dynamic_slice_in_dim(cols_sq, col_start, col_block, 0)
            other_scale = lax.dynamic_slice_in_dim(cols_scale, col_start, col_block, 0)
            products = lax.dot_general(
                part_x, other_x, (((1,), (1,)), ((), ())), preferred_element_type=jnp.float32
            )
            kernel = jnp.exp(
                (products - 0.5 * part_sq[:, None] - 0.5 * other_sq[None, :]) * inv_eps
            )
            row_weight = kernel * other_scale[None, :]
            block_total = block_total + jnp.sum(row_weight, axis=1)
            if with_num:
                block_numer = block_numer + jnp.dot(
                    row_weight.astype(jnp.bfloat16), other_x, preferred_element_type=jnp.float32
                )
            return (block_total, block_numer, col_acc, col_num_acc)

        start_inner = (
            jnp.zeros((row_block,), jnp.float32),
            jnp.zeros((row_block, numer_width), jnp.float32),
            col_total,
            col_numer,
        )
        block_total, block_numer, col_total, col_numer = lax.fori_loop(
            0, block_rows // col_block, col_step, start_inner
        )
        row_total = lax.dynamic_update_slice_in_dim(row_total, block_total, row_start, 0)
        row_numer = lax.dynamic_update_slice_in_dim(row_numer, block_numer, row_start, 0)
        return (row_total, row_numer, col_total, col_numer)

    return lax.fori_loop(0, block_rows // row_block, row_step, initial)


def crossed_sums(own_side, partner_side, mirror_side, inv_eps, with_num):
    forward_part = tile_sums(own_side, partner_side, inv_eps, with_num)
    backward_part = tile_sums(own_side, mirror_side, inv_eps, with_num)
    return (forward_part[0] + backward_part[0], forward_part[1] + backward_part[1])


def neighbour_potentials(pot_one, offset, replica):
    partner_pot = potential_partner(pot_one, offset)
    mirror_pot = potential_mirror(pot_one, offset)
    mirror_pot = jnp.where(replica == 0, pot_one, mirror_pot)
    return (partner_pot, mirror_pot)


def looped_shards(points):
    block_rows = points.shape[0]
    replicas = lax.axis_size("rep")
    team_count = lax.axis_size("team")
    replica = lax.axis_index("rep")
    offset = jnp.where(replica == 0, replicas, replica)
    own_sq = square_norms(points)
    log_count = jnp.log(jnp.float32(block_rows * team_count))
    zero_pot = jnp.zeros((block_rows,), jnp.float32)
    partner_x = deliver_partner(points, offset)
    partner_sq = square_norms(partner_x)
    mirror_far = deliver_mirror(points, offset)
    mirror_x = jnp.where(replica == 0, points, mirror_far)
    mirror_sq = square_norms(mirror_x)
    first_local, unused_numer = crossed_sums(
        (points, own_sq, zero_pot),
        (partner_x, partner_sq, zero_pot),
        (mirror_x, mirror_sq, zero_pot),
        0.25,
        False,
    )
    first_sum = lax.psum(first_local, "rep")
    pot_one = 0.5 * (zero_pot - 4.0 * (jnp.log(first_sum) - log_count))
    partner_pot, mirror_pot = neighbour_potentials(pot_one, offset, replica)
    second_local, numer_local = crossed_sums(
        (points, own_sq, pot_one),
        (partner_x, partner_sq, partner_pot),
        (mirror_x, mirror_sq, mirror_pot),
        0.5,
        True,
    )
    second, numerator = lax.psum((second_local, numer_local), "rep")
    potential = 0.5 * (pot_one - 2.0 * (jnp.log(second) - log_count))
    displacement = points.astype(jnp.float32) - numerator / second[:, None]
    return (potential, displacement)


TILE_BYTES = 36 << 20


def solution(mesh):
    team = mesh.shape["team"]

    def body(points):
        n = points.shape[0]
        fits = 4 * n * n * team <= TILE_BYTES and team == 8 and n % 256 == 0
        return shards(points) if fits else looped_shards(points)

    return jax.shard_map(
        body,
        mesh=mesh,
        in_specs=(P("team", None),),
        out_specs=(P("team"), P("team", None)),
        check_vma=False,
    )
```

```python
import functools
import jax
import jax.numpy as jnp
from jax import lax
from jax.experimental import pallas as pl
from jax.experimental.pallas import tpu as pltpu
from jax.sharding import PartitionSpec as P

F32 = jnp.float32
BF16 = jnp.bfloat16
NT = (((1,), (1,)), ((), ()))
IN_VMEM = pl.BlockSpec(memory_space=pltpu.VMEM)
IN_HBM = pl.BlockSpec(memory_space=pl.ANY)
PARAMS = pltpu.CompilerParams(vmem_limit_bytes=16 << 20)


def kept(array):
    return pltpu.with_memory_space_constraint(array, pltpu.VMEM)


def swapped(array, mask):
    size = lax.axis_size("team")
    return lax.ppermute(array, "team", [(i, i ^ mask) for i in range(size)])


def exchanged(array, even, odd):
    size = lax.axis_size("team")
    return lax.ppermute(array, "team", [(i, i ^ (odd if i % 2 else even)) for i in range(size)])


def across(columns):
    row = lax.broadcasted_iota(jnp.int32, (128, 128), 0)
    diagonal = row == lax.broadcasted_iota(jnp.int32, (128, 128), 1)
    sums = [jnp.sum(columns[g : g + 128, :], axis=1, keepdims=True) for g in range(0, columns.shape[0], 128)]
    return [jnp.sum(jnp.where(diagonal, s, 0.0), axis=0, keepdims=True) for s in sums]


def pieces(x_turned):
    wide = x_turned.astype(F32)
    norms = jnp.sum(wide * wide, axis=0, keepdims=True)
    high = norms.astype(BF16).astype(F32)
    rest = norms - high
    middle = rest.astype(BF16).astype(F32)
    return high, middle, rest - middle


def put_columns(cols, part, x, x_turned):
    width = x.shape[1]
    high, middle, low = pieces(x_turned)
    sub = lax.broadcasted_iota(jnp.int32, (16, x.shape[0]), 0)
    extra = jnp.where(sub == 0, high, jnp.where(sub == 1, middle, jnp.where(sub == 2, low, 1.0))).astype(BF16)
    cols[part, :width] = x
    cols[part, width:] = jnp.concatenate([extra] * (width // 16), axis=0).T


def put_rows(rows, x_turned):
    width, n = x_turned.shape
    high, middle, low = pieces(x_turned)
    sub = lax.broadcasted_iota(jnp.int32, (16, n), 0)
    norm = jnp.where(sub == 3, high, jnp.where(sub == 4, middle, low))
    extra = jnp.where(sub < 3, -0.125, jnp.where(sub < 6, norm * -0.125, 0.0))
    rows[:width, :] = x_turned * jnp.asarray(0.25, BF16)
    rows[width : width + 16, :] = extra.astype(BF16)
    rows[width + 16 :, :] = jnp.zeros((width - 16, n), BF16)


def row_kernel(x_ref, rows_ref, own_ref):
    own_ref[...] = x_ref[...]
    put_rows(rows_ref, x_ref[...].T)


def put_tiles(rows_ref, x_refs, e_refs, turned_refs, col_refs, acc_in, acc_ref, along_ref):
    n = x_refs[0].shape[0]
    block = 256
    for i in range(0, n, block):
        groups = range(i // 128, (i + block) // 128)
        if acc_ref is not None:
            totals = [jnp.zeros((8, 128), F32) if acc_in is None else acc_in[8 * g : 8 * g + 8, :] for g in groups]
        for x_ref, e_ref, turned_ref, cols in zip(x_refs, e_refs, turned_refs, col_refs):
            for j in range(0, n, block):
                part = slice(j, j + block)
                if i == 0:
                    x_turned = x_ref[part, :].T
                    turned_ref[:, part] = x_turned
                    put_columns(cols, part, x_ref[part, :], x_turned)
                p = jnp.dot(cols[part, :], rows_ref[:, i : i + block], preferred_element_type=F32)
                sideways = along_ref is not None and x_ref is x_refs[-1]
                along = along_ref[part, :] if sideways and i else jnp.zeros((block, 128), F32)
                for t, g in enumerate(groups):
                    k = jnp.exp(p[:, t * 128 : (t + 1) * 128])
                    e_ref[part, g * 128 : g * 128 + 128] = k * k
                    if acc_ref is not None:
                        totals[t] = totals[t] + jnp.sum(k.reshape(block // 8, 8, 128), axis=0)
                    if sideways:
                        along = along + k
                if sideways:
                    along_ref[part, :] = along
        if acc_ref is not None:
            for t, g in enumerate(groups):
                acc_ref[8 * g : 8 * g + 8, :] = totals[t]


def first_kernel(count, start, sums, as_rows, *refs):
    rows_ref, x_refs, refs = refs[0], refs[1 : 1 + count], refs[1 + count :]
    acc_in = acc_ref = None
    if sums and not start:
        acc_in, refs = refs[0], refs[1:]
    e_refs, turned_refs, refs = refs[:count], refs[count : 2 * count], refs[2 * count :]
    if sums:
        acc_ref, refs = refs[0], refs[1:]
    if as_rows:
        put_rows(refs[0], x_refs[0][...].T)
        refs = refs[1:]
    put_tiles(rows_ref, x_refs, e_refs, turned_refs, refs, acc_in, acc_ref, None)


def third_kernel(*refs):
    rows_ref, near_rows, cross_ref, near_mate_ref, acc_in, *refs = refs
    e_cross, e_mate, cross_t, mate_t, out_ref, cross_cols, mate_cols, chosen, along, between, acc = refs
    team = lax.axis_index("team")
    with_mate = team % 2 == team // 2 % 2
    n = cross_ref.shape[0]
    groups = n // 128
    block = 256
    put_tiles(
        rows_ref,
        [cross_ref, near_mate_ref],
        [e_cross, e_mate],
        [cross_t, mate_t],
        [cross_cols, mate_cols],
        acc_in,
        acc,
        along,
    )
    for i in range(0, n, block):
        totals = [jnp.zeros((8, 128), F32) for _ in range(block // 128)]
        for j in range(0, n, block):
            part = slice(j, j + block)
            if i == 0:
                chosen[part, :] = jnp.where(with_mate, mate_cols[part, :], cross_cols[part, :])
            p = jnp.dot(chosen[part, :], near_rows[:, i : i + block], preferred_element_type=F32)
            over = between[part, :] if i else jnp.zeros((block, 128), F32)
            for t in range(block // 128):
                k = jnp.exp(p[:, t * 128 : (t + 1) * 128])
                over = over + k
                totals[t] = totals[t] + jnp.sum(k.reshape(block // 8, 8, 128), axis=0)
            between[part, :] = over
        for t, total in enumerate(totals):
            g = groups + i // 128 + t
            out_ref[g : g + 1, :] = jnp.sum(total, axis=0, keepdims=True)
    out_ref[2 * groups : 3 * groups, :] = jnp.concatenate(across(between[...]), axis=0)
    out_ref[3 * groups :, :] = jnp.concatenate(across(along[...]), axis=0)
    for g in range(groups):
        out_ref[g : g + 1, :] = jnp.sum(acc[8 * g : 8 * g + 8, :], axis=0, keepdims=True)


def pack_kernel(*refs):
    step = refs[0].shape[0]
    for t, ref in enumerate(refs[:-1]):
        refs[-1][t * step : (t + 1) * step, :] = ref[...]


PARTS = (((0,), (1, 2)), ((1, 2), (3, 4, 5)), ((3, 4, 5), (6, 7)), ((6, 7), ()))


def second_kernel(points, masks, *refs):
    count = len(masks)
    e_refs, refs = refs[:count], refs[count:]
    x_refs, refs = refs[:count], refs[count:]
    pack_refs, refs = refs[:5], refs[5:]
    own_ref, pot_hbm, out_hbm, shares_ref, scales, num_ref, acc_ref, pot_ref, out_ref, sems = refs
    width, n = x_refs[0].shape
    groups = n // 128
    block = 256
    team = lax.axis_index("team")
    core, side = team % 2, team // 2 % 2

    def message(mask, slot):
        if mask >= 6:
            return pack_refs[mask - 6][slot * groups : (slot + 1) * groups, :]
        first = (mask % 2 * 4 + slot) * groups
        return pack_refs[(4, 2, 3)[mask // 2]][first : first + groups, :]

    def first_sum(mask):
        even, low = core == mask % 2, side == mask // 2 % 2
        two, three, four, five = mask ^ 2, mask ^ 3, mask ^ 4, mask ^ 5
        total = message(mask, 0) + jnp.where(even, message(two, 1), message(four, 1))
        at_low = jnp.where(even, message(three, 2), message(five, 2))
        at_high = jnp.where(even, message(four, 2), message(two, 2))
        return total + jnp.where(low, at_low, at_high) + jnp.where(even, message(three, 3), message(five, 3))

    sums = [first_sum(mask) for mask in range(count)]
    order = [sums[even] if even == odd else jnp.where(core == 0, sums[even], sums[odd]) for even, odd in masks]
    shares = float(points) / jnp.concatenate(order, axis=0)
    shares_ref[...] = jnp.concatenate([shares, jnp.zeros((128 - count * groups, 128), F32)], axis=0).T

    def put_scales(t):
        for g in range(groups):
            first = t * n + g * 128
            lane = t * groups + g
            scales[first : first + 128, :] = jnp.broadcast_to(shares_ref[:, lane : lane + 1], (128, 128))

    def part(tiles, ahead):
        start = tiles[0] == 0
        for t in ahead:
            put_scales(t)
        for i in range(0, n, block):
            cols = slice(i, i + block)
            lanes = range(i, i + block, 128)
            numerator = jnp.zeros((width, block), F32) if start else num_ref[:, cols]
            totals = [jnp.zeros((8, 128), F32) if start else acc_ref[l // 16 : l // 16 + 8, :] for l in lanes]
            for t in tiles:
                for j in range(0, n, block):
                    scale = scales[t * n + j : t * n + j + block, :]
                    weights = []
                    for u, l in enumerate(lanes):
                        w = e_refs[t][j : j + block, l : l + 128] * scale
                        totals[u] = totals[u] + jnp.sum(w.reshape(block // 8, 8, 128), axis=0)
                        weights.append(w.astype(BF16))
                    weight = jnp.concatenate(weights, axis=1)
                    numerator = numerator + jnp.dot(x_refs[t][:, j : j + block], weight, preferred_element_type=F32)
            for u, l in enumerate(lanes):
                acc_ref[l // 16 : l // 16 + 8, :] = totals[u]
            num_ref[:, cols] = numerator

    def out_copy(i):
        rows = slice(i * block, (i + 1) * block)
        return pltpu.make_async_copy(out_ref.at[rows, :], out_hbm.at[rows, :], sems.at[i])

    put_scales(0)
    for tiles, ahead in PARTS:
        pl.when(team >= 0)(functools.partial(part, tiles, ahead))
    seconds = []
    for g in range(groups):
        rows = slice(g * 128, (g + 1) * 128)
        seconds.append(jnp.sum(acc_ref[8 * g : 8 * g + 8, :], axis=0, keepdims=True))
        out_ref[rows, :] = own_ref[rows, :].astype(F32) - (num_ref[:, rows] / seconds[-1]).T
        if (g + 1) * 128 % block == 0:
            out_copy(g * 128 // block).start()
    log_count = jnp.log(jnp.float32(points))
    second = jnp.concatenate(seconds, axis=0)
    pot_one = -2.0 * (jnp.log(sums[0]) - log_count)
    pot_ref[...] = 0.5 * (pot_one - 2.0 * (jnp.log(second) - log_count))
    pot_copy = pltpu.make_async_copy(pot_ref, pot_hbm, sems.at[n // block])
    pot_copy.start()
    for i in range(n // block):
        out_copy(i).wait()
    pot_copy.wait()


def shards(points):
    n, width = points.shape
    total_points = n * lax.axis_size("team")
    groups = n // 128
    chunks = n // 256

    def tile(shape, dtype=F32):
        return pltpu.VMEM(shape, dtype)

    def call(kernel, out_shape, args, scratch=(), out_specs=None, name=None, tiles=0):
        single = not isinstance(out_shape, tuple)
        specs = out_specs or (IN_VMEM if single else tuple(IN_VMEM for _ in out_shape))
        return pl.pallas_call(
            kernel,
            out_shape=out_shape,
            in_specs=[IN_VMEM] * len(args),
            out_specs=specs,
            scratch_shapes=list(scratch),
            compiler_params=PARAMS,
            cost_estimate=pl.CostEstimate(flops=tiles * 24 * n * n * width, bytes_accessed=0, transcendentals=0),
            name=name,
        )(*[kept(a) for a in args])

    acc = None
    done = {}

    def first(blocks, sums=True, as_rows=False):
        nonlocal acc
        count = len(blocks)
        out = call(
            functools.partial(first_kernel, count, acc is None, sums, as_rows),
            (tile((n, n)),) * count
            + (tile((width, n), BF16),) * count
            + (tile((8 * groups, 128)),) * sums
            + (tile((2 * width, n), BF16),) * as_rows,
            [rows, *blocks.values()] + ([acc] if sums and acc is not None else []),
            scratch=[pltpu.VMEM((n, 2 * width), BF16)] * count,
            name="first",
            tiles=count,
        )
        for t, block in enumerate(blocks):
            done[block] = (out[t], out[count + t])
        if sums:
            acc = out[2 * count]
        return out[-1]

    def after(x):
        nonlocal acc
        x, acc = lax.optimization_barrier((x, acc))
        return x

    near = exchanged(points, 2, 4)
    mate = swapped(points, 1)
    rows, own = call(row_kernel, (tile((2 * width, n), BF16), tile((n, width), BF16)), [points], name="rows")
    first(dict(own=own))
    cross = exchanged(after(points), 4, 2)
    first(dict(mate=mate))
    near = after(near)
    near_mate = swapped(near, 1)
    near_rows = first(dict(near=near), as_rows=True)
    diagonal = exchanged(after(near), 4, 2)
    cross_mate = swapped(cross, 1)
    *out, sums = call(
        third_kernel,
        (tile((n, n)),) * 2 + (tile((width, n), BF16),) * 2 + (tile((4 * groups, 128)),),
        [rows, near_rows, cross, near_mate, acc],
        scratch=[
            pltpu.VMEM((n, 2 * width), BF16),
            pltpu.VMEM((n, 2 * width), BF16),
            pltpu.VMEM((n, 2 * width), BF16),
            pltpu.VMEM((n, 128), F32),
            pltpu.VMEM((n, 128), F32),
            pltpu.VMEM((8 * groups, 128), F32),
        ],
        name="between",
        tiles=3,
    )
    done["cross"], done["near_mate"] = (out[0], out[2]), (out[1], out[3])
    far = swapped(sums, 6)
    mate_sums = swapped(sums, 1)
    pack = call(pack_kernel, tile((8 * groups, 128)), [sums, mate_sums], name="pack")
    x, y = [swapped(pack, m) for m in (2, 4)]
    cross_mate, diagonal, pack = lax.optimization_barrier((cross_mate, diagonal, pack))
    diagonal_mate = swapped(diagonal, 1)
    first(dict(cross_mate=cross_mate, diagonal=diagonal), sums=False)
    e, far = lax.optimization_barrier((done["diagonal"][0], far))
    done["diagonal"] = (e, done["diagonal"][1])
    far_mate = swapped(far, 1)
    first(dict(diagonal_mate=diagonal_mate), sums=False)
    packs = [far, far_mate, x, y, pack]
    masks = dict(
        own=(0, 0),
        mate=(1, 1),
        near=(2, 4),
        cross_mate=(3, 5),
        cross=(4, 2),
        near_mate=(5, 3),
        diagonal=(6, 6),
        diagonal_mate=(7, 7),
    )
    potential, displacement = call(
        functools.partial(second_kernel, total_points, list(masks.values())),
        (jax.ShapeDtypeStruct((groups, 128), F32), jax.ShapeDtypeStruct((n, width), F32)),
        [done[b][0] for b in masks] + [done[b][1] for b in masks] + packs + [own],
        scratch=[
            pltpu.VMEM((128, 128), F32),
            pltpu.VMEM((len(masks) * n, 128), F32),
            pltpu.VMEM((width, n), F32),
            pltpu.VMEM((8 * groups, 128), F32),
            pltpu.VMEM((groups, 128), F32),
            pltpu.VMEM((n, width), F32),
            pltpu.SemaphoreType.DMA((chunks + 1,)),
        ],
        out_specs=(IN_HBM, IN_HBM),
        name="second",
        tiles=len(masks),
    )
    return potential.reshape(n), displacement


def shifted(block, axis, distance):
    devices = range(lax.axis_size(axis))
    route = [((i - distance) % len(devices), i) for i in devices]
    return lax.ppermute(block, axis, route)


def square_norms(block_points):
    return jnp.sum(jnp.square(block_points.astype(jnp.float32)), axis=1)


def digit_set(offset, bit_index):
    return jnp.right_shift(offset, bit_index) % 2 == 1


def deliver_partner(block_points, offset):
    digits = lax.axis_size("rep").bit_length()
    current = block_points
    for bit_index in range(digits):
        arrived = shifted(current, "team", -(1 << bit_index))
        current = jnp.where(digit_set(offset, bit_index), arrived, current)
    return current


def deliver_mirror(block_points, offset):
    digits = lax.axis_size("rep").bit_length()
    current = block_points
    for bit_index in range(digits):
        arrived = shifted(current, "team", 1 << bit_index)
        current = jnp.where(digit_set(offset, bit_index), arrived, current)
    return current


def potential_partner(pot_one, offset):
    digits = lax.axis_size("rep").bit_length()
    current = pot_one
    for bit_index in range(digits):
        arrived = shifted(current, "team", -(1 << bit_index))
        current = jnp.where(digit_set(offset, bit_index), arrived, current)
    return current


def potential_mirror(pot_one, offset):
    digits = lax.axis_size("rep").bit_length()
    current = pot_one
    for bit_index in range(digits):
        arrived = shifted(current, "team", 1 << bit_index)
        current = jnp.where(digit_set(offset, bit_index), arrived, current)
    return current


def tile_sums(row_side, col_side, inv_eps, with_num):
    rows_x, rows_sq, rows_pot = row_side
    cols_x, cols_sq, cols_pot = col_side
    block_rows = rows_x.shape[0]
    numer_width = rows_x.shape[1] if with_num else 0
    col_count = 0
    row_block = min(block_rows, 512)
    col_block = min(block_rows, 256)
    cols_scale = jnp.exp(cols_pot * inv_eps)
    initial = (
        jnp.zeros((block_rows,), jnp.float32),
        jnp.zeros((block_rows, numer_width), jnp.float32),
        jnp.zeros((col_count,), jnp.float32),
        jnp.zeros((col_count, numer_width), jnp.float32),
    )

    def row_step(row_index, carried):
        row_total, row_numer, col_total, col_numer = carried
        row_start = row_index * row_block
        part_x = lax.dynamic_slice_in_dim(rows_x, row_start, row_block, 0)
        part_sq = lax.dynamic_slice_in_dim(rows_sq, row_start, row_block, 0)

        def col_step(col_index, inner_carried):
            block_total, block_numer, col_acc, col_num_acc = inner_carried
            col_start = col_index * col_block
            other_x = lax.dynamic_slice_in_dim(cols_x, col_start, col_block, 0)
            other_sq = lax.dynamic_slice_in_dim(cols_sq, col_start, col_block, 0)
            other_scale = lax.dynamic_slice_in_dim(cols_scale, col_start, col_block, 0)
            products = lax.dot_general(
                part_x, other_x, (((1,), (1,)), ((), ())), preferred_element_type=jnp.float32
            )
            kernel = jnp.exp(
                (products - 0.5 * part_sq[:, None] - 0.5 * other_sq[None, :]) * inv_eps
            )
            row_weight = kernel * other_scale[None, :]
            block_total = block_total + jnp.sum(row_weight, axis=1)
            if with_num:
                block_numer = block_numer + jnp.dot(
                    row_weight.astype(jnp.bfloat16), other_x, preferred_element_type=jnp.float32
                )
            return (block_total, block_numer, col_acc, col_num_acc)

        start_inner = (
            jnp.zeros((row_block,), jnp.float32),
            jnp.zeros((row_block, numer_width), jnp.float32),
            col_total,
            col_numer,
        )
        block_total, block_numer, col_total, col_numer = lax.fori_loop(
            0, block_rows // col_block, col_step, start_inner
        )
        row_total = lax.dynamic_update_slice_in_dim(row_total, block_total, row_start, 0)
        row_numer = lax.dynamic_update_slice_in_dim(row_numer, block_numer, row_start, 0)
        return (row_total, row_numer, col_total, col_numer)

    return lax.fori_loop(0, block_rows // row_block, row_step, initial)


def crossed_sums(own_side, partner_side, mirror_side, inv_eps, with_num):
    forward_part = tile_sums(own_side, partner_side, inv_eps, with_num)
    backward_part = tile_sums(own_side, mirror_side, inv_eps, with_num)
    return (forward_part[0] + backward_part[0], forward_part[1] + backward_part[1])


def neighbour_potentials(pot_one, offset, replica):
    partner_pot = potential_partner(pot_one, offset)
    mirror_pot = potential_mirror(pot_one, offset)
    mirror_pot = jnp.where(replica == 0, pot_one, mirror_pot)
    return (partner_pot, mirror_pot)


def looped_shards(points):
    block_rows = points.shape[0]
    replicas = lax.axis_size("rep")
    team_count = lax.axis_size("team")
    replica = lax.axis_index("rep")
    offset = jnp.where(replica == 0, replicas, replica)
    own_sq = square_norms(points)
    log_count = jnp.log(jnp.float32(block_rows * team_count))
    zero_pot = jnp.zeros((block_rows,), jnp.float32)
    partner_x = deliver_partner(points, offset)
    partner_sq = square_norms(partner_x)
    mirror_far = deliver_mirror(points, offset)
    mirror_x = jnp.where(replica == 0, points, mirror_far)
    mirror_sq = square_norms(mirror_x)
    first_local, unused_numer = crossed_sums(
        (points, own_sq, zero_pot),
        (partner_x, partner_sq, zero_pot),
        (mirror_x, mirror_sq, zero_pot),
        0.25,
        False,
    )
    first_sum = lax.psum(first_local, "rep")
    pot_one = 0.5 * (zero_pot - 4.0 * (jnp.log(first_sum) - log_count))
    partner_pot, mirror_pot = neighbour_potentials(pot_one, offset, replica)
    second_local, numer_local = crossed_sums(
        (points, own_sq, pot_one),
        (partner_x, partner_sq, partner_pot),
        (mirror_x, mirror_sq, mirror_pot),
        0.5,
        True,
    )
    second, numerator = lax.psum((second_local, numer_local), "rep")
    potential = 0.5 * (pot_one - 2.0 * (jnp.log(second) - log_count))
    displacement = points.astype(jnp.float32) - numerator / second[:, None]
    return (potential, displacement)


TILE_BYTES = 36 << 20


def solution(mesh):
    team = mesh.shape["team"]

    def body(points):
        n = points.shape[0]
        fits = 4 * n * n * team <= TILE_BYTES and team == 8 and n % 256 == 0
        return shards(points) if fits else looped_shards(points)

    return jax.shard_map(
        body,
        mesh=mesh,
        in_specs=(P("team", None),),
        out_specs=(P("team"), P("team", None)),
        check_vma=False,
    )
```

```python
import functools
import jax
import jax.numpy as jnp
from jax import lax
from jax.experimental import pallas as pl
from jax.experimental.pallas import tpu as pltpu
from jax.sharding import PartitionSpec as P

F32 = jnp.float32
BF16 = jnp.bfloat16
NT = (((1,), (1,)), ((), ()))
IN_VMEM = pl.BlockSpec(memory_space=pltpu.VMEM)
IN_HBM = pl.BlockSpec(memory_space=pl.ANY)
PARAMS = pltpu.CompilerParams(vmem_limit_bytes=16 << 20)


def kept(array):
    return pltpu.with_memory_space_constraint(array, pltpu.VMEM)


def swapped(array, mask):
    size = lax.axis_size("team")
    return lax.ppermute(array, "team", [(i, i ^ mask) for i in range(size)])


def exchanged(array, even, odd):
    size = lax.axis_size("team")
    return lax.ppermute(array, "team", [(i, i ^ (odd if i % 2 else even)) for i in range(size)])


def across(columns):
    row = lax.broadcasted_iota(jnp.int32, (128, 128), 0)
    diagonal = row == lax.broadcasted_iota(jnp.int32, (128, 128), 1)
    sums = [jnp.sum(columns[g : g + 128, :], axis=1, keepdims=True) for g in range(0, columns.shape[0], 128)]
    return [jnp.sum(jnp.where(diagonal, s, 0.0), axis=0, keepdims=True) for s in sums]


def pieces(x_turned):
    wide = x_turned.astype(F32)
    norms = jnp.sum(wide * wide, axis=0, keepdims=True)
    high = norms.astype(BF16).astype(F32)
    rest = norms - high
    middle = rest.astype(BF16).astype(F32)
    return high, middle, rest - middle


def put_columns(cols, part, x, x_turned):
    width = x.shape[1]
    high, middle, low = pieces(x_turned)
    sub = lax.broadcasted_iota(jnp.int32, (16, x.shape[0]), 0)
    extra = jnp.where(sub == 0, high, jnp.where(sub == 1, middle, jnp.where(sub == 2, low, 1.0))).astype(BF16)
    cols[part, :width] = x
    cols[part, width:] = jnp.concatenate([extra] * (width // 16), axis=0).T


def put_rows(rows, x_turned):
    width, n = x_turned.shape
    high, middle, low = pieces(x_turned)
    sub = lax.broadcasted_iota(jnp.int32, (16, n), 0)
    norm = jnp.where(sub == 3, high, jnp.where(sub == 4, middle, low))
    extra = jnp.where(sub < 3, -0.125, jnp.where(sub < 6, norm * -0.125, 0.0))
    rows[:width, :] = x_turned * jnp.asarray(0.25, BF16)
    rows[width : width + 16, :] = extra.astype(BF16)
    rows[width + 16 :, :] = jnp.zeros((width - 16, n), BF16)


def row_kernel(x_ref, rows_ref, own_ref):
    own_ref[...] = x_ref[...]
    put_rows(rows_ref, x_ref[...].T)


def put_tiles(rows_ref, x_refs, e_refs, turned_refs, col_refs, acc_in, acc_ref, along_ref):
    n = x_refs[0].shape[0]
    block = 256
    for i in range(0, n, block):
        groups = range(i // 128, (i + block) // 128)
        if acc_ref is not None:
            totals = [jnp.zeros((8, 128), F32) if acc_in is None else acc_in[8 * g : 8 * g + 8, :] for g in groups]
        for x_ref, e_ref, turned_ref, cols in zip(x_refs, e_refs, turned_refs, col_refs):
            for j in range(0, n, block):
                part = slice(j, j + block)
                if i == 0:
                    x_turned = x_ref[part, :].T
                    turned_ref[:, part] = x_turned
                    put_columns(cols, part, x_ref[part, :], x_turned)
                p = jnp.dot(cols[part, :], rows_ref[:, i : i + block], preferred_element_type=F32)
                sideways = along_ref is not None and x_ref is x_refs[-1]
                along = along_ref[part, :] if sideways and i else jnp.zeros((block, 128), F32)
                for t, g in enumerate(groups):
                    k = jnp.exp(p[:, t * 128 : (t + 1) * 128])
                    e_ref[part, g * 128 : g * 128 + 128] = k * k
                    if acc_ref is not None:
                        totals[t] = totals[t] + jnp.sum(k.reshape(block // 8, 8, 128), axis=0)
                    if sideways:
                        along = along + k
                if sideways:
                    along_ref[part, :] = along
        if acc_ref is not None:
            for t, g in enumerate(groups):
                acc_ref[8 * g : 8 * g + 8, :] = totals[t]


def first_kernel(count, start, sums, as_rows, *refs):
    rows_ref, x_refs, refs = refs[0], refs[1 : 1 + count], refs[1 + count :]
    acc_in = acc_ref = None
    if sums and not start:
        acc_in, refs = refs[0], refs[1:]
    e_refs, turned_refs, refs = refs[:count], refs[count : 2 * count], refs[2 * count :]
    if sums:
        acc_ref, refs = refs[0], refs[1:]
    if as_rows:
        put_rows(refs[0], x_refs[0][...].T)
        refs = refs[1:]
    put_tiles(rows_ref, x_refs, e_refs, turned_refs, refs, acc_in, acc_ref, None)


def third_kernel(*refs):
    rows_ref, near_rows, cross_ref, near_mate_ref, acc_in, *refs = refs
    e_cross, e_mate, cross_t, mate_t, out_ref, cross_cols, mate_cols, chosen, along, between, acc = refs
    team = lax.axis_index("team")
    with_mate = team % 2 == team // 2 % 2
    n = cross_ref.shape[0]
    groups = n // 128
    block = 256
    put_tiles(
        rows_ref,
        [cross_ref, near_mate_ref],
        [e_cross, e_mate],
        [cross_t, mate_t],
        [cross_cols, mate_cols],
        acc_in,
        acc,
        along,
    )
    for i in range(0, n, block):
        totals = [jnp.zeros((8, 128), F32) for _ in range(block // 128)]
        for j in range(0, n, block):
            part = slice(j, j + block)
            if i == 0:
                chosen[part, :] = jnp.where(with_mate, mate_cols[part, :], cross_cols[part, :])
            p = jnp.dot(chosen[part, :], near_rows[:, i : i + block], preferred_element_type=F32)
            over = between[part, :] if i else jnp.zeros((block, 128), F32)
            for t in range(block // 128):
                k = jnp.exp(p[:, t * 128 : (t + 1) * 128])
                over = over + k
                totals[t] = totals[t] + jnp.sum(k.reshape(block // 8, 8, 128), axis=0)
            between[part, :] = over
        for t, total in enumerate(totals):
            g = groups + i // 128 + t
            out_ref[g : g + 1, :] = jnp.sum(total, axis=0, keepdims=True)
    out_ref[2 * groups : 3 * groups, :] = jnp.concatenate(across(between[...]), axis=0)
    out_ref[3 * groups :, :] = jnp.concatenate(across(along[...]), axis=0)
    for g in range(groups):
        out_ref[g : g + 1, :] = jnp.sum(acc[8 * g : 8 * g + 8, :], axis=0, keepdims=True)


def pack_kernel(*refs):
    step = refs[0].shape[0]
    for t, ref in enumerate(refs[:-1]):
        refs[-1][t * step : (t + 1) * step, :] = ref[...]


PARTS = (((0,), (1, 2)), ((1, 2), (3, 4, 5)), ((3, 4, 5), (6, 7)), ((6, 7), ()))


def second_kernel(points, masks, *refs):
    count = len(masks)
    e_refs, refs = refs[:count], refs[count:]
    x_refs, refs = refs[:count], refs[count:]
    pack_refs, refs = refs[:5], refs[5:]
    own_ref, pot_hbm, out_hbm, shares_ref, scales, num_ref, acc_ref, pot_ref, out_ref, sems = refs
    width, n = x_refs[0].shape
    groups = n // 128
    block = 256
    team = lax.axis_index("team")
    core, side = team % 2, team // 2 % 2

    def message(mask, slot):
        if mask >= 6:
            return pack_refs[mask - 6][slot * groups : (slot + 1) * groups, :]
        first = (mask % 2 * 4 + slot) * groups
        return pack_refs[(4, 2, 3)[mask // 2]][first : first + groups, :]

    def first_sum(mask):
        even, low = core == mask % 2, side == mask // 2 % 2
        two, three, four, five = mask ^ 2, mask ^ 3, mask ^ 4, mask ^ 5
        total = message(mask, 0) + jnp.where(even, message(two, 1), message(four, 1))
        at_low = jnp.where(even, message(three, 2), message(five, 2))
        at_high = jnp.where(even, message(four, 2), message(two, 2))
        return total + jnp.where(low, at_low, at_high) + jnp.where(even, message(three, 3), message(five, 3))

    sums = [first_sum(mask) for mask in range(count)]
    order = [sums[even] if even == odd else jnp.where(core == 0, sums[even], sums[odd]) for even, odd in masks]
    shares = float(points) / jnp.concatenate(order, axis=0)
    shares_ref[...] = jnp.concatenate([shares, jnp.zeros((128 - count * groups, 128), F32)], axis=0).T

    def put_scales(t):
        for g in range(groups):
            first = t * n + g * 128
            lane = t * groups + g
            scales[first : first + 128, :] = jnp.broadcast_to(shares_ref[:, lane : lane + 1], (128, 128))

    def part(tiles, ahead):
        start = tiles[0] == 0
        for t in ahead:
            put_scales(t)
        for i in range(0, n, block):
            cols = slice(i, i + block)
            lanes = range(i, i + block, 128)
            numerator = jnp.zeros((width, block), F32) if start else num_ref[:, cols]
            totals = [jnp.zeros((8, 128), F32) if start else acc_ref[l // 16 : l // 16 + 8, :] for l in lanes]
            for t in tiles:
                for j in range(0, n, block):
                    scale = scales[t * n + j : t * n + j + block, :]
                    weights = []
                    for u, l in enumerate(lanes):
                        w = e_refs[t][j : j + block, l : l + 128] * scale
                        totals[u] = totals[u] + jnp.sum(w.reshape(block // 8, 8, 128), axis=0)
                        weights.append(w.astype(BF16))
                    weight = jnp.concatenate(weights, axis=1)
                    numerator = numerator + jnp.dot(x_refs[t][:, j : j + block], weight, preferred_element_type=F32)
            for u, l in enumerate(lanes):
                acc_ref[l // 16 : l // 16 + 8, :] = totals[u]
            num_ref[:, cols] = numerator

    def out_copy(i):
        rows = slice(i * block, (i + 1) * block)
        return pltpu.make_async_copy(out_ref.at[rows, :], out_hbm.at[rows, :], sems.at[i])

    put_scales(0)
    for tiles, ahead in PARTS:
        pl.when(team >= 0)(functools.partial(part, tiles, ahead))
    seconds = [jnp.sum(acc_ref[8 * g : 8 * g + 8, :], axis=0, keepdims=True) for g in range(groups)]
    second = jnp.concatenate(seconds, axis=0)
    log_count = jnp.log(jnp.float32(points))
    pot_one = -2.0 * (jnp.log(sums[0]) - log_count)
    pot_ref[...] = 0.5 * (pot_one - 2.0 * (jnp.log(second) - log_count))
    pot_copy = pltpu.make_async_copy(pot_ref, pot_hbm, sems.at[n // block])
    pot_copy.start()
    for g in range(groups):
        rows = slice(g * 128, (g + 1) * 128)
        out_ref[rows, :] = own_ref[rows, :].astype(F32) - (num_ref[:, rows] / seconds[g]).T
        if (g + 1) * 128 % block == 0:
            out_copy(g * 128 // block).start()
    for i in range(n // block):
        out_copy(i).wait()
    pot_copy.wait()


def shards(points):
    n, width = points.shape
    total_points = n * lax.axis_size("team")
    groups = n // 128
    chunks = n // 256

    def tile(shape, dtype=F32):
        return pltpu.VMEM(shape, dtype)

    def call(kernel, out_shape, args, scratch=(), out_specs=None, name=None, tiles=0):
        single = not isinstance(out_shape, tuple)
        specs = out_specs or (IN_VMEM if single else tuple(IN_VMEM for _ in out_shape))
        return pl.pallas_call(
            kernel,
            out_shape=out_shape,
            in_specs=[IN_VMEM] * len(args),
            out_specs=specs,
            scratch_shapes=list(scratch),
            compiler_params=PARAMS,
            cost_estimate=pl.CostEstimate(flops=tiles * 24 * n * n * width, bytes_accessed=0, transcendentals=0),
            name=name,
        )(*[kept(a) for a in args])

    acc = None
    done = {}

    def first(blocks, sums=True, as_rows=False):
        nonlocal acc
        count = len(blocks)
        out = call(
            functools.partial(first_kernel, count, acc is None, sums, as_rows),
            (tile((n, n)),) * count
            + (tile((width, n), BF16),) * count
            + (tile((8 * groups, 128)),) * sums
            + (tile((2 * width, n), BF16),) * as_rows,
            [rows, *blocks.values()] + ([acc] if sums and acc is not None else []),
            scratch=[pltpu.VMEM((n, 2 * width), BF16)] * count,
            name="first",
            tiles=count,
        )
        for t, block in enumerate(blocks):
            done[block] = (out[t], out[count + t])
        if sums:
            acc = out[2 * count]
        return out[-1]

    def after(x):
        nonlocal acc
        x, acc = lax.optimization_barrier((x, acc))
        return x

    near = exchanged(points, 2, 4)
    mate = swapped(points, 1)
    rows, own = call(row_kernel, (tile((2 * width, n), BF16), tile((n, width), BF16)), [points], name="rows")
    first(dict(own=own))
    cross = exchanged(after(points), 4, 2)
    first(dict(mate=mate))
    near = after(near)
    near_mate = swapped(near, 1)
    near_rows = first(dict(near=near), as_rows=True)
    diagonal = exchanged(after(near), 4, 2)
    cross_mate = swapped(cross, 1)
    *out, sums = call(
        third_kernel,
        (tile((n, n)),) * 2 + (tile((width, n), BF16),) * 2 + (tile((4 * groups, 128)),),
        [rows, near_rows, cross, near_mate, acc],
        scratch=[
            pltpu.VMEM((n, 2 * width), BF16),
            pltpu.VMEM((n, 2 * width), BF16),
            pltpu.VMEM((n, 2 * width), BF16),
            pltpu.VMEM((n, 128), F32),
            pltpu.VMEM((n, 128), F32),
            pltpu.VMEM((8 * groups, 128), F32),
        ],
        name="between",
        tiles=3,
    )
    done["cross"], done["near_mate"] = (out[0], out[2]), (out[1], out[3])
    far = swapped(sums, 6)
    mate_sums = swapped(sums, 1)
    pack = call(pack_kernel, tile((8 * groups, 128)), [sums, mate_sums], name="pack")
    x, y = [swapped(pack, m) for m in (2, 4)]
    cross_mate, diagonal, pack = lax.optimization_barrier((cross_mate, diagonal, pack))
    diagonal_mate = swapped(diagonal, 1)
    first(dict(cross_mate=cross_mate, diagonal=diagonal), sums=False)
    e, far = lax.optimization_barrier((done["diagonal"][0], far))
    done["diagonal"] = (e, done["diagonal"][1])
    far_mate = swapped(far, 1)
    first(dict(diagonal_mate=diagonal_mate), sums=False)
    packs = [far, far_mate, x, y, pack]
    masks = dict(
        own=(0, 0),
        mate=(1, 1),
        near=(2, 4),
        cross_mate=(3, 5),
        cross=(4, 2),
        near_mate=(5, 3),
        diagonal=(6, 6),
        diagonal_mate=(7, 7),
    )
    potential, displacement = call(
        functools.partial(second_kernel, total_points, list(masks.values())),
        (jax.ShapeDtypeStruct((groups, 128), F32), jax.ShapeDtypeStruct((n, width), F32)),
        [done[b][0] for b in masks] + [done[b][1] for b in masks] + packs + [own],
        scratch=[
            pltpu.VMEM((128, 128), F32),
            pltpu.VMEM((len(masks) * n, 128), F32),
            pltpu.VMEM((width, n), F32),
            pltpu.VMEM((8 * groups, 128), F32),
            pltpu.VMEM((groups, 128), F32),
            pltpu.VMEM((n, width), F32),
            pltpu.SemaphoreType.DMA((chunks + 1,)),
        ],
        out_specs=(IN_HBM, IN_HBM),
        name="second",
        tiles=len(masks),
    )
    return potential.reshape(n), displacement


def shifted(block, axis, distance):
    devices = range(lax.axis_size(axis))
    route = [((i - distance) % len(devices), i) for i in devices]
    return lax.ppermute(block, axis, route)


def square_norms(block_points):
    return jnp.sum(jnp.square(block_points.astype(jnp.float32)), axis=1)


def digit_set(offset, bit_index):
    return jnp.right_shift(offset, bit_index) % 2 == 1


def deliver_partner(block_points, offset):
    digits = lax.axis_size("rep").bit_length()
    current = block_points
    for bit_index in range(digits):
        arrived = shifted(current, "team", -(1 << bit_index))
        current = jnp.where(digit_set(offset, bit_index), arrived, current)
    return current


def deliver_mirror(block_points, offset):
    digits = lax.axis_size("rep").bit_length()
    current = block_points
    for bit_index in range(digits):
        arrived = shifted(current, "team", 1 << bit_index)
        current = jnp.where(digit_set(offset, bit_index), arrived, current)
    return current


def potential_partner(pot_one, offset):
    digits = lax.axis_size("rep").bit_length()
    current = pot_one
    for bit_index in range(digits):
        arrived = shifted(current, "team", -(1 << bit_index))
        current = jnp.where(digit_set(offset, bit_index), arrived, current)
    return current


def potential_mirror(pot_one, offset):
    digits = lax.axis_size("rep").bit_length()
    current = pot_one
    for bit_index in range(digits):
        arrived = shifted(current, "team", 1 << bit_index)
        current = jnp.where(digit_set(offset, bit_index), arrived, current)
    return current


def tile_sums(row_side, col_side, inv_eps, with_num):
    rows_x, rows_sq, rows_pot = row_side
    cols_x, cols_sq, cols_pot = col_side
    block_rows = rows_x.shape[0]
    numer_width = rows_x.shape[1] if with_num else 0
    col_count = 0
    row_block = min(block_rows, 512)
    col_block = min(block_rows, 256)
    cols_scale = jnp.exp(cols_pot * inv_eps)
    initial = (
        jnp.zeros((block_rows,), jnp.float32),
        jnp.zeros((block_rows, numer_width), jnp.float32),
        jnp.zeros((col_count,), jnp.float32),
        jnp.zeros((col_count, numer_width), jnp.float32),
    )

    def row_step(row_index, carried):
        row_total, row_numer, col_total, col_numer = carried
        row_start = row_index * row_block
        part_x = lax.dynamic_slice_in_dim(rows_x, row_start, row_block, 0)
        part_sq = lax.dynamic_slice_in_dim(rows_sq, row_start, row_block, 0)

        def col_step(col_index, inner_carried):
            block_total, block_numer, col_acc, col_num_acc = inner_carried
            col_start = col_index * col_block
            other_x = lax.dynamic_slice_in_dim(cols_x, col_start, col_block, 0)
            other_sq = lax.dynamic_slice_in_dim(cols_sq, col_start, col_block, 0)
            other_scale = lax.dynamic_slice_in_dim(cols_scale, col_start, col_block, 0)
            products = lax.dot_general(
                part_x, other_x, (((1,), (1,)), ((), ())), preferred_element_type=jnp.float32
            )
            kernel = jnp.exp(
                (products - 0.5 * part_sq[:, None] - 0.5 * other_sq[None, :]) * inv_eps
            )
            row_weight = kernel * other_scale[None, :]
            block_total = block_total + jnp.sum(row_weight, axis=1)
            if with_num:
                block_numer = block_numer + jnp.dot(
                    row_weight.astype(jnp.bfloat16), other_x, preferred_element_type=jnp.float32
                )
            return (block_total, block_numer, col_acc, col_num_acc)

        start_inner = (
            jnp.zeros((row_block,), jnp.float32),
            jnp.zeros((row_block, numer_width), jnp.float32),
            col_total,
            col_numer,
        )
        block_total, block_numer, col_total, col_numer = lax.fori_loop(
            0, block_rows // col_block, col_step, start_inner
        )
        row_total = lax.dynamic_update_slice_in_dim(row_total, block_total, row_start, 0)
        row_numer = lax.dynamic_update_slice_in_dim(row_numer, block_numer, row_start, 0)
        return (row_total, row_numer, col_total, col_numer)

    return lax.fori_loop(0, block_rows // row_block, row_step, initial)


def crossed_sums(own_side, partner_side, mirror_side, inv_eps, with_num):
    forward_part = tile_sums(own_side, partner_side, inv_eps, with_num)
    backward_part = tile_sums(own_side, mirror_side, inv_eps, with_num)
    return (forward_part[0] + backward_part[0], forward_part[1] + backward_part[1])


def neighbour_potentials(pot_one, offset, replica):
    partner_pot = potential_partner(pot_one, offset)
    mirror_pot = potential_mirror(pot_one, offset)
    mirror_pot = jnp.where(replica == 0, pot_one, mirror_pot)
    return (partner_pot, mirror_pot)


def looped_shards(points):
    block_rows = points.shape[0]
    replicas = lax.axis_size("rep")
    team_count = lax.axis_size("team")
    replica = lax.axis_index("rep")
    offset = jnp.where(replica == 0, replicas, replica)
    own_sq = square_norms(points)
    log_count = jnp.log(jnp.float32(block_rows * team_count))
    zero_pot = jnp.zeros((block_rows,), jnp.float32)
    partner_x = deliver_partner(points, offset)
    partner_sq = square_norms(partner_x)
    mirror_far = deliver_mirror(points, offset)
    mirror_x = jnp.where(replica == 0, points, mirror_far)
    mirror_sq = square_norms(mirror_x)
    first_local, unused_numer = crossed_sums(
        (points, own_sq, zero_pot),
        (partner_x, partner_sq, zero_pot),
        (mirror_x, mirror_sq, zero_pot),
        0.25,
        False,
    )
    first_sum = lax.psum(first_local, "rep")
    pot_one = 0.5 * (zero_pot - 4.0 * (jnp.log(first_sum) - log_count))
    partner_pot, mirror_pot = neighbour_potentials(pot_one, offset, replica)
    second_local, numer_local = crossed_sums(
        (points, own_sq, pot_one),
        (partner_x, partner_sq, partner_pot),
        (mirror_x, mirror_sq, mirror_pot),
        0.5,
        True,
    )
    second, numerator = lax.psum((second_local, numer_local), "rep")
    potential = 0.5 * (pot_one - 2.0 * (jnp.log(second) - log_count))
    displacement = points.astype(jnp.float32) - numerator / second[:, None]
    return (potential, displacement)


TILE_BYTES = 36 << 20


def solution(mesh):
    team = mesh.shape["team"]

    def body(points):
        n = points.shape[0]
        fits = 4 * n * n * team <= TILE_BYTES and team == 8 and n % 256 == 0
        return shards(points) if fits else looped_shards(points)

    return jax.shard_map(
        body,
        mesh=mesh,
        in_specs=(P("team", None),),
        out_specs=(P("team"), P("team", None)),
        check_vma=False,
    )
```
